256 devices in a mesh: blk: 256 (over z, y, x, core).
Axes of the slice: x: 4, y: 4, z: 8, core: 2. Of those that a mesh axis runs over, the one named last changes fastest.
Arguments:
- frames: bfloat16 [131072, 1536], P('blk'), may hold values from -6 to 6
- head: bfloat16 [1536, 768], replicated, may hold values from -0.15625 to 0.15625
- offsets: int32 [131072], P('blk'), may hold values from 1 to 1024, as said below
Outputs:
- losses: float32 [131072], P('blk')
- frame_grad: bfloat16 [131072, 1536], P('blk')
- head_grad: bfloat16 [1536, 768], replicated
The draws below stay inside these ranges and needn't reach their ends.
Inputs may be any that keep to these rules, and one draw needn't show every extreme that they name: `offsets`: the positive of row i is row (i + offsets_i) mod 131072, always a later frame within 1024 rows.
All inputs are finite; a program needn't handle non-finite values.
Results may differ from the reference program's by a relative error of at most 0.0061.
Values may be sent and summed in bfloat16 or wider, within the bound.
No kernel may reach another device: no remote copies, remote signals or barrier semaphores. Data moves between devices by JAX's collectives and lax.ppermute only.
A program may use at most 64 MiB of HBM per device.

```python
import jax
import jax.numpy as jnp
from jax import lax

D = 1536
P_SIZE = 768
ROWS = 512
REACH = 2
TOKENS = 131072


def draw_offsets(key, part):
    key = jax.random.fold_in(key, 7)
    values = jax.random.randint(key, (TOKENS,), 1, REACH * ROWS + 1, dtype=jnp.int32)
    values = values.at[0].set(REACH * ROWS)
    values = values.at[1].set(1)
    return values


def steps_of(key, shape, split, least, high):
    level, own = 1.0, jax.random.fold_in(key, 6)
    for dim, blocks in split:
        draws = jnp.exp(jax.random.uniform(jax.random.fold_in(own, dim), (blocks,), jnp.float32, least / len(split), high / len(split)))
        level = level * jnp.repeat(draws, shape[dim] // blocks).reshape([-1 if axis == dim else 1 for axis in range(len(shape))])
    return level


def gaussian(rng, extent, deviation, limit, shards=(), held_as=jnp.bfloat16):
    values = jax.random.normal(rng, extent, jnp.float32) * deviation
    if len(shards) > 0:
        values = steps_of(rng, extent, shards, -0.22, 0.18) * values
    return jnp.clip(values, min=-limit, max=limit).astype(held_as)


def setup_inputs(seed: int = 0) -> dict:
    seeds = jax.random.split(jax.random.key(seed), 4)
    frames = gaussian(seeds[0], (TOKENS, D), 1.0, 6.0, ((0, 256),))
    head = gaussian(seeds[1], (D, P_SIZE), D ** -0.5, 0.15625)
    offsets = draw_offsets(jax.random.fold_in(seeds[3], 71), 0)
    return {"frames": frames, "head": head, "offsets": offsets}


sharpness_scale = 50.0

def quantized_quantity(value):
    return lax.optimization_barrier(value.astype(jnp.bfloat16)).astype(jnp.float32)

def reference(frames, head, offsets):
    nblocks = TOKENS // ROWS
    z = jnp.dot(frames, head, preferred_element_type=jnp.float32)
    norm = jnp.sqrt(lax.optimization_barrier(jnp.sum(z * z, axis=1, keepdims=True)) + 1e-06)
    unit = z / norm
    mapped_feature_vector = unit.astype(jnp.bfloat16)
    clip_segments = mapped_feature_vector.reshape(nblocks, ROWS, P_SIZE)
    shifts = [0] + list(range(1, REACH + 1)) + [-k for k in range(1, REACH + 1)]
    order = jnp.array(shifts, jnp.int32)
    block_offsets = offsets.reshape(nblocks, ROWS)
    rowids = jnp.arange(ROWS, dtype=jnp.int32)
    colids = jnp.arange((2 * REACH + 1) * ROWS, dtype=jnp.int32)
    diag = colids[None, :] == rowids[:, None]

    def first(segment_index):
        ids = (segment_index + order) % nblocks
        vertical_elements = clip_segments[ids].reshape(-1, P_SIZE)
        cosine_affinity = sharpness_scale * jnp.dot(clip_segments[segment_index], vertical_elements.T, preferred_element_type=jnp.float32)
        onehot = colids[None, :] == (rowids + block_offsets[segment_index])[:, None]
        expd = jnp.where(diag, 0.0, jnp.exp(cosine_affinity))
        lse = jnp.log(lax.optimization_barrier(jnp.sum(expd, axis=1)))
        loss = lse - lax.optimization_barrier(jnp.sum(jnp.where(onehot, cosine_affinity, 0.0), axis=1))
        probs = jnp.where(diag, 0.0, jnp.exp(cosine_affinity - lse[:, None]))
        grad = (probs - onehot.astype(jnp.float32)).astype(jnp.bfloat16)
        return (loss, grad)
    losses, grads = lax.map(first, jnp.arange(nblocks, dtype=jnp.int32))

    def second(segment_index):
        current_segment = clip_segments[segment_index]
        grad = grads[segment_index]
        selfpair_logit_patch = grad[:, :ROWS]
        overall_aggregate = sharpness_scale * (jnp.dot(selfpair_logit_patch, current_segment, preferred_element_type=jnp.float32) + jnp.dot(selfpair_logit_patch.T, current_segment, preferred_element_type=jnp.float32))
        for neighborhood_position in range(1, 2 * REACH + 1):
            shift = shifts[neighborhood_position]
            other = (segment_index + shift) % nblocks
            companion_segment = clip_segments[other]
            mirror_slot = neighborhood_position + REACH if shift > 0 else neighborhood_position - REACH
            logit_array_patch = grad[:, neighborhood_position * ROWS:(neighborhood_position + 1) * ROWS]
            later_adjacent_segment = quantized_quantity(sharpness_scale * jnp.dot(logit_array_patch, companion_segment, preferred_element_type=jnp.float32))
            earlier_logit_patch = grads[other][:, mirror_slot * ROWS:(mirror_slot + 1) * ROWS]
            earlier_adjacent_segment = quantized_quantity(sharpness_scale * jnp.dot(earlier_logit_patch.T, companion_segment, preferred_element_type=jnp.float32))
            overall_aggregate = overall_aggregate + later_adjacent_segment + earlier_adjacent_segment
        return overall_aggregate
    feature_derivative = lax.map(second, jnp.arange(nblocks, dtype=jnp.int32)).reshape(TOKENS, P_SIZE)
    dz = ((feature_derivative - unit * lax.optimization_barrier(jnp.sum(unit * feature_derivative, axis=1, keepdims=True))) / norm).astype(jnp.bfloat16)
    frame_grad = jnp.dot(dz, head.T, preferred_element_type=jnp.float32).astype(jnp.bfloat16)
    head_grad = jnp.dot(frames.T, dz, preferred_element_type=jnp.float32).astype(jnp.bfloat16)
    return (losses.reshape(TOKENS), frame_grad, head_grad)
```

```python
import jax
import jax.numpy as jnp
from jax import lax
from jax.sharding import Mesh, PartitionSpec as P

SCALE = 50.0
ALL = ("z", "y", "x", "core")
SIZES = (8, 4, 4, 2)
F32, BF16 = jnp.float32, jnp.bfloat16


def send(x, to):
    return lax.ppermute(x, ALL, [(i, to(i) % 256) for i in range(256)])


def in_chip(x):
    return send(x, lambda i: i ^ 1)


def ahead(x, by):
    return send(x, lambda i: i + by)


def along(x, axis, by):
    n = lax.axis_size(axis)
    return lax.ppermute(x, axis, [(i, (i + by) % n) for i in range(n)])


def dot(left, right):
    return jnp.dot(left, right, preferred_element_type=F32)


def dot_nt(left, right):
    return lax.dot_general(left, right, (((1,), (1,)), ((), ())), preferred_element_type=F32)


def dot_tn(left, right):
    return lax.dot_general(left, right, (((0,), (0,)), ((), ())), preferred_element_type=F32)


def rows_at(x, start, size):
    return lax.dynamic_slice_in_dim(x, start, size, 0)


def scatter_sum(part, axis):
    n, me = lax.axis_size(axis), lax.axis_index(axis)
    size = part.shape[0] // n
    got = [
        along(rows_at(part, (me + r) % n * size, size).astype(BF16), axis, r) for r in range(1, n)
    ]
    total = rows_at(part, me * size, size).astype(F32)
    for g in got:
        total = total + g.astype(F32)
    return total


def gather(piece, axis):
    n, me = lax.axis_size(axis), lax.axis_index(axis)
    size = piece.shape[0]
    whole = jnp.zeros((n * size,) + piece.shape[1:], piece.dtype)
    whole = lax.dynamic_update_slice_in_dim(whole, piece, me * size, 0)
    for r in range(1, n):
        whole = lax.dynamic_update_slice_in_dim(
            whole, along(piece, axis, r), (me - r + n) % n * size, 0
        )
    return whole


def on_device(frames, head, offsets):
    rows, depth = frames.shape
    width = head.shape[1]
    core = lax.axis_index("core")
    even = core == 0
    z = dot(frames, head)
    norm = jnp.sqrt(jnp.sum(z * z, axis=1, keepdims=True) + 1e-06)
    unit = z / norm
    emb = unit.astype(BF16)

    swapped = in_chip(emb)
    first = send(emb, lambda i: i - 2 if i % 2 == 0 else i + 2)
    second = send(emb, lambda i: i + 2 if i % 2 == 0 else i - 2)
    relayed = in_chip(first)
    blocks = [emb, swapped, first, relayed, second]
    place = [0, jnp.where(even, 1, -1), jnp.where(even, 2, -2), jnp.where(even, -1, 1), jnp.where(even, -2, 2)]

    half = depth // 2
    mine = lax.dynamic_slice_in_dim(frames, core * half, half, 1)
    theirs = in_chip(lax.dynamic_slice_in_dim(frames, (1 - core) * half, half, 1))

    rowids = jnp.arange(rows, dtype=jnp.int32)
    target = rowids + offsets
    back1, back2 = ahead(target, 1), ahead(target, 2)
    exps, total, score_pos = [], jnp.zeros((rows,), F32), jnp.zeros((rows,), F32)
    for block, at in zip(blocks, place):
        score = SCALE * dot_nt(emb, block)
        hit = (rowids + at * rows)[None, :] == target[:, None]
        score_pos = score_pos + jnp.sum(jnp.where(hit, score, 0.0), axis=1)
        e = jnp.exp(score)
        if block is emb:
            e = jnp.where(rowids[None, :] == rowids[:, None], 0.0, e)
        total = total + jnp.sum(e, axis=1)
        exps.append(e)
    losses = jnp.log(total) - score_pos
    inv = 1.0 / total
    b1, b2, f1, f2 = ahead(inv, 1), ahead(inv, 2), ahead(inv, -1), ahead(inv, -2)
    invs = [inv, jnp.where(even, f1, b1), jnp.where(even, f2, b2), jnp.where(even, b1, f1), jnp.where(even, b2, f2)]
    never = jnp.full_like(target, -1)
    targets = [
        target,
        jnp.where(even, never, back1 - rows),
        jnp.where(even, never, back2 - 2 * rows),
        jnp.where(even, back1 - rows, never),
        jnp.where(even, back2 - 2 * rows, never),
    ]
    demb = jnp.zeros((rows, width), F32)
    for block, at, e, other, goal in zip(blocks, place, exps, invs, targets):
        hit = (rowids + at * rows)[None, :] == target[:, None]
        hit_back = rowids[:, None] == goal[None, :]
        g = e * (inv[:, None] + other[None, :]) - hit.astype(F32) - hit_back.astype(F32)
        demb = demb + dot(g.astype(BF16), block)
    demb = SCALE * demb
    dz = ((demb - unit * jnp.sum(unit * demb, axis=1, keepdims=True)) / norm).astype(BF16)
    frame_grad = dot_nt(dz, head).astype(BF16)

    dz_other = in_chip(dz)
    part = dot_tn(mine, dz) + dot_tn(theirs, dz_other)
    cut = width // 2
    left = scatter_sum(scatter_sum(part[:, :cut], "x"), "y")
    right = scatter_sum(scatter_sum(part[:, cut:], "y"), "x")
    both = scatter_sum(jnp.concatenate([left, right], axis=1), "z").astype(BF16)
    both = gather(both, "z")
    left = gather(gather(both[:, :cut], "y"), "x")
    right = gather(gather(both[:, cut:], "x"), "y")
    own = jnp.concatenate([left, right], axis=1)
    peer = in_chip(own)
    head_grad = jnp.concatenate([jnp.where(even, own, peer), jnp.where(even, peer, own)], axis=0)
    return (losses, frame_grad, head_grad)


def solution(mesh):
    torus = Mesh(mesh.devices.reshape(SIZES), ALL)
    return jax.shard_map(
        on_device,
        mesh=torus,
        in_specs=(P(ALL, None), P(), P(ALL)),
        out_specs=(P(ALL), P(ALL, None), P()),
        check_vma=False,
    )
```

```python
import jax
import jax.numpy as jnp
from jax import lax
from jax.sharding import Mesh, PartitionSpec as P

SCALE = 50.0
ALL = ("z", "y", "x", "core")
SIZES = (8, 4, 4, 2)
F32, BF16 = jnp.float32, jnp.bfloat16


def send(x, to):
    return lax.ppermute(x, ALL, [(i, to(i) % 256) for i in range(256)])


def in_chip(x):
    return send(x, lambda i: i ^ 1)


def ahead(x, by):
    return send(x, lambda i: i + by)


def dot(left, right):
    return jnp.dot(left, right, preferred_element_type=F32)


def dot_nt(left, right):
    return lax.dot_general(left, right, (((1,), (1,)), ((), ())), preferred_element_type=F32)


def dot_tn(left, right):
    return lax.dot_general(left, right, (((0,), (0,)), ((), ())), preferred_element_type=F32)


def scatter_sum(part, axes):
    n = lax.axis_size(axes)
    shares = part.astype(BF16).reshape(n, part.shape[0] // n, part.shape[1])
    got = lax.all_to_all(shares, axes, split_axis=0, concat_axis=0)
    return jnp.sum(got.astype(F32), axis=0)


def gather(piece, axes):
    n = lax.axis_size(axes)
    copies = jnp.broadcast_to(piece[None], (n,) + piece.shape)
    got = lax.all_to_all(copies, axes, split_axis=0, concat_axis=0)
    return got.reshape((n * piece.shape[0],) + piece.shape[1:])


def on_device(frames, head, offsets):
    rows, depth = frames.shape
    width = head.shape[1]
    core = lax.axis_index("core")
    even = core == 0
    z = dot(frames, head)
    norm = jnp.sqrt(jnp.sum(z * z, axis=1, keepdims=True) + 1e-06)
    unit = z / norm
    emb = unit.astype(BF16)

    swapped = in_chip(emb)
    first = send(emb, lambda i: i - 2 if i % 2 == 0 else i + 2)
    second = send(emb, lambda i: i + 2 if i % 2 == 0 else i - 2)
    relayed = in_chip(first)
    blocks = [emb, swapped, first, relayed, second]
    place = [0, jnp.where(even, 1, -1), jnp.where(even, 2, -2), jnp.where(even, -1, 1), jnp.where(even, -2, 2)]

    half = depth // 2
    mine = lax.dynamic_slice_in_dim(frames, core * half, half, 1)
    theirs = in_chip(lax.dynamic_slice_in_dim(frames, (1 - core) * half, half, 1))

    rowids = jnp.arange(rows, dtype=jnp.int32)
    target = rowids + offsets
    exps, total, score_pos = [], jnp.zeros((rows,), F32), jnp.zeros((rows,), F32)
    for block, at in zip(blocks, place):
        score = SCALE * dot_nt(emb, block)
        hit = (rowids + at * rows)[None, :] == target[:, None]
        score_pos = score_pos + jnp.sum(jnp.where(hit, score, 0.0), axis=1)
        e = jnp.exp(score)
        if block is emb:
            e = jnp.where(rowids[None, :] == rowids[:, None], 0.0, e)
        total = total + jnp.sum(e, axis=1)
        exps.append(e)
    losses = jnp.log(total) - score_pos
    inv = 1.0 / total
    note = jnp.stack([inv, target.astype(F32)])
    peer_note = in_chip(note)
    pair = jnp.concatenate([jnp.where(even, note, peer_note), jnp.where(even, peer_note, note)])
    behind, beyond = ahead(pair, 2), ahead(pair, -2)
    b1, b2 = jnp.where(even, behind[2:], peer_note), jnp.where(even, behind[:2], behind[2:])
    f1, f2 = jnp.where(even, peer_note[0], beyond[0]), jnp.where(even, beyond[0], beyond[2])
    back1, back2 = b1[1].astype(jnp.int32), b2[1].astype(jnp.int32)
    b1, b2 = b1[0], b2[0]
    invs = [inv, jnp.where(even, f1, b1), jnp.where(even, f2, b2), jnp.where(even, b1, f1), jnp.where(even, b2, f2)]
    never = jnp.full_like(target, -1)
    targets = [
        target,
        jnp.where(even, never, back1 - rows),
        jnp.where(even, never, back2 - 2 * rows),
        jnp.where(even, back1 - rows, never),
        jnp.where(even, back2 - 2 * rows, never),
    ]
    demb = jnp.zeros((rows, width), F32)
    for block, at, e, other, goal in zip(blocks, place, exps, invs, targets):
        hit = (rowids + at * rows)[None, :] == target[:, None]
        hit_back = rowids[:, None] == goal[None, :]
        g = e * (inv[:, None] + other[None, :]) - hit.astype(F32) - hit_back.astype(F32)
        demb = demb + dot(g.astype(BF16), block)
    demb = SCALE * demb
    dz = ((demb - unit * jnp.sum(unit * demb, axis=1, keepdims=True)) / norm).astype(BF16)
    frame_grad = dot_nt(dz, head).astype(BF16)

    dz_other = in_chip(dz)
    part = dot_tn(mine, dz) + dot_tn(theirs, dz_other)
    share = scatter_sum(scatter_sum(part, ("y", "x")), "z").astype(BF16)
    own = gather(gather(share, "z"), ("y", "x"))
    peer = in_chip(own)
    head_grad = jnp.concatenate([jnp.where(even, own, peer), jnp.where(even, peer, own)], axis=0)
    return (losses, frame_grad, head_grad)


def solution(mesh):
    torus = Mesh(mesh.devices.reshape(SIZES), ALL)
    return jax.shard_map(
        on_device,
        mesh=torus,
        in_specs=(P(ALL, None), P(), P(ALL)),
        out_specs=(P(ALL), P(ALL, None), P()),
        check_vma=False,
    )
```

```python
import jax
import jax.numpy as jnp
from jax import lax
from jax.experimental import pallas as pl
from jax.experimental.pallas import tpu as pltpu
from jax.sharding import Mesh, PartitionSpec as P

SCALE = 50.0
ALL = ("z", "y", "x", "core")
SIZES = (8, 4, 4, 2)
F32, BF16 = jnp.float32, jnp.bfloat16
TILE = 128


def send(x, to):
    return lax.ppermute(x, ALL, [(i, to(i) % 256) for i in range(256)])


def in_chip(x):
    return send(x, lambda i: i ^ 1)


def inward(x):
    return send(x, lambda i: i - 2 if i % 2 == 0 else i + 2)


def outward(x):
    return send(x, lambda i: i + 2 if i % 2 == 0 else i - 2)


def dot(left, right):
    return jnp.dot(left, right, preferred_element_type=F32)


def dot_nt(left, right):
    return lax.dot_general(left, right, (((1,), (1,)), ((), ())), preferred_element_type=F32)


def to_row(column):
    return jnp.broadcast_to(column, (column.shape[0], 128)).T[:1]


def to_column(row):
    return jnp.broadcast_to(row, (128, row.shape[1])).T[:, :1]


def call(body, out, scalars, *arrays, scratch=(), flops=0, name=None):
    vmem = pl.BlockSpec(memory_space=pltpu.VMEM)
    smem = pl.BlockSpec(memory_space=pltpu.SMEM)
    size = sum(a.size * a.dtype.itemsize for a in (*arrays, *out))
    specs = [smem] * len(scalars) + [vmem] * len(arrays)
    return pl.pallas_call(
        body,
        out_shape=out,
        in_specs=specs,
        out_specs=[vmem] * len(out),
        scratch_shapes=scratch,
        name=name,
        compiler_params=pltpu.CompilerParams(vmem_limit_bytes=16 * 2**20),
        cost_estimate=pl.CostEstimate(flops=flops, bytes_accessed=size, transcendentals=0),
    )(*scalars, *arrays)


def after(x, *others):
    anywhere = pl.BlockSpec(memory_space=pl.ANY)
    return pl.pallas_call(
        lambda *refs: None,
        out_shape=jax.ShapeDtypeStruct(x.shape, x.dtype),
        in_specs=[anywhere] * (1 + len(others)),
        out_specs=anywhere,
        input_output_aliases={0: 0},
        name="after",
        compiler_params=pltpu.CompilerParams(vmem_limit_bytes=2**20),
    )(x, *others)


def embed(frames, head, emb, unit, rnorm, acc):
    k = pl.program_id(0)

    @pl.when(k == 0)
    def _():
        acc[...] = dot(frames[...], head[...])

    @pl.when(k > 0)
    def _():
        acc[...] += dot(frames[...], head[...])

    @pl.when(k == pl.num_programs(0) - 1)
    def _():
        for r in range(0, acc.shape[0], TILE):
            rows = pl.ds(r, TILE)
            z = acc[rows, :]
            norm = jnp.sqrt(jnp.sum(z * z, axis=1, keepdims=True) + 1e-06)
            inverse = 1.0 / norm
            u = z * inverse
            unit[rows, :] = u
            emb[rows, :] = u.astype(BF16)
            rnorm[rows, :] = inverse


def score_tile(at, emb, block, goal, rows):
    score = SCALE * dot_nt(emb[rows, :], block[...])
    cols = lax.broadcasted_iota(jnp.int32, score.shape, 1) + at * block.shape[0]
    hit = cols == goal[rows, :]
    return score, jnp.sum(jnp.where(hit, score, 0.0), axis=1, keepdims=True)


def near(at, emb, peer, goal, e_own, e_peer, total, pos):
    for r in range(0, emb.shape[0], TILE):
        rows = pl.ds(r, TILE)
        score, p0 = score_tile(0, emb, emb, goal, rows)
        e = jnp.exp(score)
        i = lax.broadcasted_iota(jnp.int32, e.shape, 0) + r
        e = jnp.where(i == lax.broadcasted_iota(jnp.int32, e.shape, 1), 0.0, e)
        e_own[rows, :] = e
        t0 = jnp.sum(e, axis=1, keepdims=True)
        score, p1 = score_tile(at[0], emb, peer, goal, rows)
        e = jnp.exp(score)
        e_peer[rows, :] = e
        total[rows, :] = t0 + jnp.sum(e, axis=1, keepdims=True)
        pos[rows, :] = p0 + p1


def across(at, emb, block, goal, total, pos, e_out, total_out, pos_out, column_sum):
    columns = jnp.zeros((1, block.shape[0]), F32)
    for r in range(0, emb.shape[0], TILE):
        rows = pl.ds(r, TILE)
        score, p = score_tile(at[0], emb, block, goal, rows)
        e = jnp.exp(score)
        e_out[rows, :] = e
        total_out[rows, :] = total[rows, :] + jnp.sum(e, axis=1, keepdims=True)
        pos_out[rows, :] = pos[rows, :] + p
        columns += jnp.sum(e, axis=0, keepdims=True)
    column_sum[...] = columns


def relayed(at, emb, block, goal, total, pos, e_out, total_out, pos_out):
    for r in range(0, emb.shape[0], TILE):
        rows = pl.ds(r, TILE)
        score, p = score_tile(at[0], emb, block, goal, rows)
        e = jnp.exp(score)
        e_out[rows, :] = e
        total_out[rows, :] = total[rows, :] + jnp.sum(e, axis=1, keepdims=True)
        pos_out[rows, :] = pos[rows, :] + p


def close(total, last_sum, goal_row, inverse, note, log_total):
    whole = to_row(total[...]) + last_sum[...]
    inv = 1.0 / whole
    note[0:1, :] = inv
    note[1:2, :] = goal_row[...].astype(F32)
    inverse[...] = to_column(inv)
    log_total[...] = jnp.log(whole)


def slope(e, at, goal, inverse, their_inverse, their_goal, rows):
    width = e.shape[1]
    i = lax.broadcasted_iota(jnp.int32, e.shape, 0) + rows.start
    j = lax.broadcasted_iota(jnp.int32, e.shape, 1) + at * width
    ours = (j == goal[rows, :]).astype(F32)
    theirs = (i == their_goal + at * width).astype(F32)
    return e * (inverse[rows, :] + their_inverse) - ours - theirs


def gather_slopes(
    at, goal, inverse, own_note, peer_note, first_note, relay_note, e0, e1, e2, e3, b0, b1, b2, b3, out, g
):
    notes = (own_note, peer_note, first_note, relay_note)
    for k, (note, e, block) in enumerate(zip(notes, (e0, e1, e2, e3), (b0, b1, b2, b3))):
        place = 0 if k == 0 else at[k - 1]
        their_inverse, their_goal = note[0:1, :], note[1:2, :].astype(jnp.int32)
        for r in range(0, e.shape[0], TILE):
            rows = pl.ds(r, TILE)
            g[rows, :] = slope(e[rows, :], place, goal, inverse, their_inverse, their_goal, rows).astype(BF16)
        if k == 0:
            out[...] = dot(g[...], block[...])
        else:
            out[...] += dot(g[...], block[...])


def finish(
    at, emb, block, goal, inverse, note, pos, log_total, unit, rnorm, part, dz, losses, g, pos_all
):
    their_inverse, their_goal = note[0:1, :], note[1:2, :].astype(jnp.int32)
    for r in range(0, emb.shape[0], TILE):
        rows = pl.ds(r, TILE)
        score, p = score_tile(at[0], emb, block, goal, rows)
        pos_all[rows, :] = pos[rows, :] + p
        g[rows, :] = slope(jnp.exp(score), at[0], goal, inverse, their_inverse, their_goal, rows).astype(BF16)
    for r in range(0, emb.shape[0], 256):
        rows = pl.ds(r, 256)
        demb = SCALE * (part[rows, :] + dot(g[rows, :], block[...]))
        u = unit[rows, :]
        along = jnp.sum(u * demb, axis=1, keepdims=True)
        dz[rows, :] = ((demb - u * along) * rnorm[rows, :]).astype(BF16)
    losses[...] = log_total[...] - to_row(pos_all[...])


def turn(core, frames, mine, theirs):
    half = mine.shape[0]
    for out, k in ((mine, core[0]), (theirs, 1 - core[0])):
        for c in range(0, half, 256):
            columns = pl.ds(pl.multiple_of(k * half + c, 128), 256)
            out[pl.ds(c, 256), :] = frames[:, columns].T


def head_own(left, dz, out):
    out[...] = dot(left[...], dz[...])


def head_both(part, left, dz, out):
    for r in range(0, out.shape[0], 256):
        rows = pl.ds(r, 256)
        out[rows, :] = (part[rows, :] + dot(left[rows, :], dz[...])).astype(BF16)


def lay_out(core, own, other, out, sems):
    half = own.shape[0]
    copies = []
    for k, src in enumerate((own, other)):
        start = pl.multiple_of((core[0] if k == 0 else 1 - core[0]) * half, half)
        copies.append(pltpu.make_async_copy(src, out.at[pl.ds(start, half), :], sems.at[k]))
    for c in copies:
        c.start()
    for c in copies:
        c.wait()


def on_device(frames, head, offsets):
    rows, depth = frames.shape
    width = head.shape[1]
    core = lax.axis_index("core")
    even = core == 0
    shape = jax.ShapeDtypeStruct
    col, row = shape((rows, 1), F32), shape((1, rows), F32)
    square, tall = shape((rows, rows), F32), shape((rows, width), F32)
    note = shape((2, rows), F32)
    block_flops = 2 * rows * rows * width
    step, half = depth // 3, depth // 2
    emb, unit, rnorm = pl.pallas_call(
        embed,
        grid=(3,),
        in_specs=[
            pl.BlockSpec((rows, step), lambda k: (0, k)),
            pl.BlockSpec((step, width), lambda k: (k, 0)),
        ],
        out_specs=[pl.BlockSpec(memory_space=pltpu.VMEM)] * 3,
        out_shape=[shape((rows, width), BF16), tall, col],
        scratch_shapes=[pltpu.VMEM((rows, width), F32)],
        name="embed",
        compiler_params=pltpu.CompilerParams(vmem_limit_bytes=16 * 2**20),
        cost_estimate=pl.CostEstimate(flops=2 * rows * depth * width, bytes_accessed=2**22, transcendentals=0),
    )(frames, head)

    target = jnp.arange(rows, dtype=jnp.int32) + offsets
    goal, goal_row = target[:, None], target[None, :]
    sign = jnp.where(even, 1, -1).astype(jnp.int32)

    def at(k):
        return (sign * k).reshape(1)

    peer = in_chip(emb)
    first = inward(emb)
    e_own, e_peer, total, pos = call(
        near, [square, square, col, col], [at(1)], emb, peer, goal, flops=2 * block_flops, name="near"
    )
    mine, theirs = call(turn, [shape((half, rows), BF16)] * 2, [core.reshape(1)], frames, name="turn")
    emb = after(emb, total)
    last = outward(emb)
    first = after(first, total, theirs)
    relay = in_chip(first)
    theirs = in_chip(theirs)
    e_first, total, pos, column_sum = call(
        across, [square, col, col, row], [at(2)], emb, first, goal, total, pos, flops=block_flops, name="across"
    )
    last_sum = outward(column_sum)
    e_relay, total, pos = call(
        relayed, [square, col, col], [at(-1)], emb, relay, goal, total, pos, flops=block_flops, name="relayed"
    )
    inverse, own_note, log_total = call(close, [col, note, row], [], total, last_sum, goal_row, name="close")
    peer_note = in_chip(own_note)
    first_note = inward(own_note)
    both = outward(jnp.concatenate([own_note, peer_note], axis=0))
    last_note, relay_note = both[:2], both[2:]
    places = jnp.concatenate([at(1), at(2), at(-1)])
    (part,) = call(
        gather_slopes, [tall], [places], goal, inverse, own_note, peer_note, first_note, relay_note,
        e_own, e_peer, e_first, e_relay, emb, peer, first, relay,
        scratch=[pltpu.VMEM((rows, rows), BF16)], flops=4 * block_flops, name="slopes",
    )
    dz, losses = call(
        finish, [shape((rows, width), BF16), row], [at(-2)], emb, last, goal, inverse, last_note, pos, log_total,
        unit, rnorm, part, scratch=[pltpu.VMEM((rows, rows), BF16), pltpu.VMEM((rows, 1), F32)],
        flops=2 * block_flops, name="finish",
    )
    dz_other = in_chip(dz)
    frame_grad = dot_nt(dz, head).astype(BF16)

    (partial,) = call(head_own, [shape((half, width), F32)], [], mine, dz, flops=2 * half * rows * width, name="head_own")
    (partial,) = call(
        head_both, [shape((half, width), BF16)], [], partial, theirs, dz_other, flops=2 * half * rows * width, name="head_both"
    )
    shares = partial.reshape(16, half // 16, width)
    got = lax.all_to_all(shares, ("y", "x"), split_axis=0, concat_axis=0)
    share = jnp.sum(got.astype(F32), axis=0).astype(BF16)
    got = lax.all_to_all(jnp.broadcast_to(share[None], (8,) + share.shape), "z", split_axis=0, concat_axis=0)
    share = jnp.sum(got.astype(F32), axis=0).astype(BF16)
    copies = jnp.broadcast_to(share[None], (16,) + share.shape)
    own = lax.all_to_all(copies, ("y", "x"), split_axis=0, concat_axis=0).reshape(half, width)
    other = in_chip(own)
    anywhere = pl.BlockSpec(memory_space=pl.ANY)
    head_grad = pl.pallas_call(
        lay_out,
        out_shape=shape((depth, width), BF16),
        in_specs=[pl.BlockSpec(memory_space=pltpu.SMEM), anywhere, anywhere],
        out_specs=anywhere,
        scratch_shapes=[pltpu.SemaphoreType.DMA((2,))],
        name="lay_out",
        compiler_params=pltpu.CompilerParams(vmem_limit_bytes=2**20),
    )(core.reshape(1), own, other)
    return (losses.reshape(rows), frame_grad, head_grad)


def solution(mesh):
    torus = Mesh(mesh.devices.reshape(SIZES), ALL)
    return jax.shard_map(
        on_device,
        mesh=torus,
        in_specs=(P(ALL, None), P(), P(ALL)),
        out_specs=(P(ALL), P(ALL, None), P()),
        check_vma=False,
    )
```

```python
import functools

import jax
import jax.numpy as jnp
from jax import lax
from jax.experimental import pallas as pl
from jax.experimental.pallas import tpu as pltpu
from jax.sharding import Mesh, PartitionSpec as P

SCALE = 50.0
ALL = ("z", "y", "x", "core")
SIZES = (8, 4, 4, 2)
F32, BF16 = jnp.float32, jnp.bfloat16
TILE, WIDE, PIECES = 128, 256, 4


def send(x, to):
    return lax.ppermute(x, ALL, [(i, to(i) % 256) for i in range(256)])


def in_chip(x):
    return send(x, lambda i: i ^ 1)


def inward(x):
    return send(x, lambda i: i - 2 if i % 2 == 0 else i + 2)


def outward(x):
    return send(x, lambda i: i + 2 if i % 2 == 0 else i - 2)


def dot(left, right):
    return jnp.dot(left, right, preferred_element_type=F32)


def dot_nt(left, right):
    return lax.dot_general(left, right, (((1,), (1,)), ((), ())), preferred_element_type=F32)


def to_row(column):
    return jnp.broadcast_to(column, (column.shape[0], 128)).T[:1]


def to_column(row):
    return jnp.broadcast_to(row, (128, row.shape[1])).T[:, :1]


def call(body, out, *arrays, scratch=(), flops=0, name=None, kept=()):
    vmem = pl.BlockSpec(memory_space=pltpu.VMEM)
    size = sum(a.size * a.dtype.itemsize for a in (*arrays, *out))
    return pl.pallas_call(
        body,
        out_shape=out,
        in_specs=[vmem] * len(arrays),
        out_specs=[vmem] * len(out),
        scratch_shapes=scratch,
        input_output_aliases=dict(kept),
        name=name,
        compiler_params=pltpu.CompilerParams(vmem_limit_bytes=16 * 2**20),
        cost_estimate=pl.CostEstimate(flops=flops, bytes_accessed=size, transcendentals=0),
    )(*arrays)


def after(x, *others):
    anywhere = pl.BlockSpec(memory_space=pl.ANY)
    return pl.pallas_call(
        lambda *refs: None,
        out_shape=jax.ShapeDtypeStruct(x.shape, x.dtype),
        in_specs=[anywhere] * (1 + len(others)),
        out_specs=anywhere,
        input_output_aliases={0: 0},
        name="after",
        compiler_params=pltpu.CompilerParams(vmem_limit_bytes=2**20),
    )(x, *others)


def embed(frames, head, offsets, emb, unit, rnorm, goal, goal_row, f, h, acc, sems):
    depth = head.shape[0]
    step = depth // PIECES
    copies = []
    for k in range(PIECES):
        cut = pl.ds(k * step, step)
        copies.append(pltpu.make_async_copy(frames.at[:, cut], f.at[:, cut], sems.at[0, k]))
        copies.append(pltpu.make_async_copy(head.at[cut, :], h.at[cut, :], sems.at[1, k]))
    for c in copies:
        c.start()
    row = offsets[...] + lax.broadcasted_iota(jnp.int32, offsets.shape, 1)
    goal_row[...] = row.astype(F32)
    goal[...] = to_column(row.astype(F32)).astype(jnp.int32)
    for k in range(PIECES):
        cut = pl.ds(k * step, step)
        copies[2 * k].wait()
        copies[2 * k + 1].wait()
        if k == 0:
            acc[...] = dot(f[:, cut], h[cut, :])
        elif k < PIECES - 1:
            acc[...] += dot(f[:, cut], h[cut, :])
    for r in range(0, acc.shape[0], WIDE):
        rows = pl.ds(r, WIDE)
        z = acc[rows, :] + dot(f[rows, cut], h[cut, :])
        norm = jnp.sqrt(jnp.sum(z * z, axis=1, keepdims=True) + 1e-06)
        inverse = 1.0 / norm
        u = z * inverse
        unit[rows, :] = u
        emb[rows, :] = u.astype(BF16)
        rnorm[rows, :] = inverse


def places():
    sign = 1 - 2 * lax.axis_index("core")
    return (0, sign, 2 * sign, -2 * sign, -sign)


def score_tile(at, emb, block, goal, rows):
    score = SCALE * dot_nt(emb[rows, :], block[...])
    cols = lax.broadcasted_iota(jnp.int32, score.shape, 1) + at * block.shape[0]
    hit = cols == goal[rows, :]
    return score, jnp.sum(jnp.where(hit, score, 0.0), axis=1, keepdims=True)


def near(emb, peer, goal, unit, rnorm, e_all, total, pos, *kept):
    at = places()
    for r in range(0, emb.shape[0], WIDE):
        rows = pl.ds(r, WIDE)
        score, p0 = score_tile(0, emb, emb, goal, rows)
        e = jnp.exp(score)
        i = lax.broadcasted_iota(jnp.int32, e.shape, 0) + r
        e = jnp.where(i == lax.broadcasted_iota(jnp.int32, e.shape, 1), 0.0, e)
        e_all[0, rows, :] = e
        total[rows, :] = jnp.sum(e, axis=1, keepdims=True)
        score, p1 = score_tile(at[1], emb, peer, goal, rows)
        e = jnp.exp(score)
        e_all[1, rows, :] = e
        total[rows, :] += jnp.sum(e, axis=1, keepdims=True)
        pos[rows, :] = p0 + p1


def add_block(slot, emb, block, goal, e_all, total, pos):
    at = places()[slot]
    for r in range(0, emb.shape[0], WIDE):
        rows = pl.ds(r, WIDE)
        score, p = score_tile(at, emb, block, goal, rows)
        e = jnp.exp(score)
        e_all[slot, rows, :] = e
        total[rows, :] += jnp.sum(e, axis=1, keepdims=True)
        pos[rows, :] += p


def far(emb, first, last, goal, e_in, total_in, pos_in, unit, rnorm, e_all, total, pos, *kept):
    add_block(2, emb, first, goal, e_all, total, pos)
    add_block(3, emb, last, goal, e_all, total, pos)


def seal(
    emb, relay, goal, goal_row, e_in, total_in, pos_in, unit, rnorm,
    e_all, total, pos, unit_out, rnorm_out, inverse, note, losses,
):
    add_block(4, emb, relay, goal, e_all, total, pos)
    whole = to_row(total[...])
    inv = 1.0 / whole
    note[0:1, :] = inv
    note[1:2, :] = goal_row[...]
    inverse[...] = to_column(inv)
    losses[...] = jnp.log(whole) - to_row(pos[...])


def slope(e, at, goal, inverse, their_inverse, their_goal, rows):
    width = e.shape[1]
    i = lax.broadcasted_iota(jnp.int32, e.shape, 0) + rows.start
    j = lax.broadcasted_iota(jnp.int32, e.shape, 1) + at * width
    ours = (j == goal[rows, :]).astype(F32)
    theirs = (i == their_goal + at * width).astype(F32)
    return e * (inverse[rows, :] + their_inverse) - ours - theirs


def finish(
    goal, inverse, own_note, peer_note, swap_a, swap_b, e_all, emb, peer, first, last, relay, unit, rnorm,
    dz, g, acc,
):
    at = places()
    matched = lax.rem(lax.axis_index("x") + lax.axis_index("core"), 2) == 0
    toward = jnp.where(matched, swap_a[...], swap_b[...])
    away = jnp.where(matched, swap_b[...], swap_a[...])
    notes = (own_note[...], peer_note[...], toward[:2], away[:2], away[2:])
    for k, (note, block) in enumerate(zip(notes, (emb, peer, first, last, relay))):
        their_inverse, their_goal = note[0:1], note[1:2].astype(jnp.int32)
        for r in range(0, g.shape[1], TILE):
            rows = pl.ds(r, TILE)
            g[k % 2, rows, :] = slope(e_all[k, rows, :], at[k], goal, inverse, their_inverse, their_goal, rows).astype(BF16)
        if k == 0:
            acc[...] = dot(g[0], block[...])
        else:
            acc[...] += dot(g[k % 2], block[...])
    for r in range(0, emb.shape[0], TILE):
        rows = pl.ds(r, TILE)
        demb = SCALE * acc[rows, :]
        u = unit[rows, :]
        along = jnp.sum(u * demb, axis=1, keepdims=True)
        dz[rows, :] = ((demb - u * along) * rnorm[rows, :]).astype(BF16)


def turn(frames, token, mine, theirs):
    half, core = mine.shape[0], lax.axis_index("core")
    for out, k in ((mine, core), (theirs, 1 - core)):
        for c in range(0, half, 256):
            columns = pl.ds(pl.multiple_of(k * half + c, 128), 256)
            out[pl.ds(c, 256), :] = frames[:, columns].T


def add_up(got, out):
    total = got[0].astype(F32)
    for k in range(1, got.shape[0]):
        total += got[k].astype(F32)
    total = total.astype(BF16)
    for k in range(out.shape[0]):
        out[k] = total


def head_own(left, dz, out):
    out[...] = dot(left[...], dz[...])


def head_both(part, left, dz, out):
    for r in range(0, out.shape[0], 256):
        rows = pl.ds(r, 256)
        out[rows, :] = (part[rows, :] + dot(left[rows, :], dz[...])).astype(BF16)


def lay_out(other, part, *rest):
    out, sem = rest[-2:]
    size, core = part.shape[0], lax.axis_index("core")
    start = pl.multiple_of((1 - core if other else core) * size, size)
    copy = pltpu.make_async_copy(part, out.at[pl.ds(start, size), :], sem)
    copy.start()
    copy.wait()


def place_half(part, *whole):
    anywhere = pl.BlockSpec(memory_space=pl.ANY)
    return pl.pallas_call(
        functools.partial(lay_out, bool(whole)),
        out_shape=jax.ShapeDtypeStruct((2 * part.shape[0], part.shape[1]), part.dtype),
        in_specs=[anywhere] * (1 + len(whole)),
        out_specs=anywhere,
        scratch_shapes=[pltpu.SemaphoreType.DMA],
        input_output_aliases={1: 0} if whole else {},
        name="lay_out",
        compiler_params=pltpu.CompilerParams(vmem_limit_bytes=2**20),
    )(part, *whole)


def on_device(frames, head, offsets):
    rows, depth = frames.shape
    width = head.shape[1]
    shape = jax.ShapeDtypeStruct
    col, row = shape((rows, 1), F32), shape((1, rows), F32)
    square, tall = shape((rows, rows), F32), shape((rows, width), F32)
    note = shape((2, rows), F32)
    block_flops = 2 * rows * rows * width
    half = depth // 2
    vmem, hbm = pl.BlockSpec(memory_space=pltpu.VMEM), pl.BlockSpec(memory_space=pltpu.HBM)
    emb, unit, rnorm, goal, goal_row = pl.pallas_call(
        embed,
        in_specs=[hbm, hbm, vmem],
        out_specs=[vmem] * 5,
        out_shape=[shape((rows, width), BF16), tall, col, shape((rows, 1), jnp.int32), row],
        scratch_shapes=[
            pltpu.VMEM((rows, depth), BF16),
            pltpu.VMEM((depth, width), BF16),
            pltpu.VMEM((rows, width), F32),
            pltpu.SemaphoreType.DMA((2, PIECES)),
        ],
        name="embed",
        compiler_params=pltpu.CompilerParams(vmem_limit_bytes=51 * 2**20),
        cost_estimate=pl.CostEstimate(flops=2 * rows * depth * width, bytes_accessed=2**22, transcendentals=0),
    )(frames, head, offsets.reshape(1, rows))

    peer = in_chip(emb)
    first = inward(emb)
    last = outward(emb)
    everything = shape((5, rows, rows), F32)
    e_all, total, pos, unit, rnorm = call(
        near, [everything, col, col, tall, col], emb, peer, goal, unit, rnorm,
        kept=((3, 3), (4, 4)), flops=2 * block_flops, name="near",
    )
    mine, theirs = call(turn, [shape((half, rows), BF16)] * 2, frames, pos, name="turn")
    first = after(first, total, theirs)
    relay = in_chip(first)
    theirs = in_chip(theirs)
    e_all, total, pos, unit, rnorm = call(
        far, [everything, col, col, tall, col], emb, first, last, goal, e_all, total, pos, unit, rnorm,
        kept=((4, 0), (5, 1), (6, 2), (7, 3), (8, 4)), flops=2 * block_flops, name="far",
    )
    e_all, total, pos, unit, rnorm, inverse, own_note, losses = call(
        seal, [everything, col, col, tall, col, col, note, row],
        emb, relay, goal, goal_row, e_all, total, pos, unit, rnorm,
        kept=((4, 0), (5, 1), (6, 2), (7, 3), (8, 4)), flops=block_flops, name="seal",
    )
    peer_note = in_chip(own_note)
    pair = jnp.concatenate([own_note, peer_note], axis=0)
    swap_a, swap_b = send(pair, lambda i: i ^ 2), send(pair, lambda i: ((i + 2) ^ 2) - 2)
    (dz,) = call(
        finish, [shape((rows, width), BF16)], goal, inverse, own_note, peer_note, swap_a, swap_b, e_all,
        emb, peer, first, last, relay, unit, rnorm,
        scratch=[pltpu.VMEM((2, rows, rows), BF16), pltpu.VMEM((rows, width), F32)],
        flops=5 * block_flops, name="finish",
    )
    dz_other = in_chip(dz)
    frame_grad = dot_nt(dz, head).astype(BF16)

    (partial,) = call(head_own, [shape((half, width), F32)], mine, dz, flops=2 * half * rows * width, name="head_own")
    (partial,) = call(
        head_both, [shape((half, width), BF16)], partial, theirs, dz_other, flops=2 * half * rows * width, name="head_both"
    )
    shares = partial.reshape(16, half // 16, width)
    got = lax.all_to_all(shares, ("y", "x"), split_axis=0, concat_axis=0)
    (copies,) = call(add_up, [shape((8, half // 16, width), BF16)], got, name="add_plane")
    got = lax.all_to_all(copies, "z", split_axis=0, concat_axis=0)
    (copies,) = call(add_up, [shape((16, half // 16, width), BF16)], got, name="add_z")
    own = lax.all_to_all(copies, ("y", "x"), split_axis=0, concat_axis=0).reshape(half, width)
    other = in_chip(own)
    head_grad = place_half(other, place_half(own))
    return (losses.reshape(rows), frame_grad, head_grad)


def solution(mesh):
    torus = Mesh(mesh.devices.reshape(SIZES), ALL)
    return jax.shard_map(
        on_device,
        mesh=torus,
        in_specs=(P(ALL, None), P(), P(ALL)),
        out_specs=(P(ALL), P(ALL, None), P()),
        check_vma=False,
    )
```

```python
import functools

import jax
import jax.numpy as jnp
from jax import lax
from jax.experimental import pallas as pl
from jax.experimental.pallas import tpu as pltpu
from jax.sharding import Mesh, PartitionSpec as P

SCALE = 50.0
ALL = ("zh", "zl", "y", "x", "core")
SIZES = (4, 2, 4, 4, 2)
NEAR = ("zl", "y", "x")
F32, BF16 = jnp.float32, jnp.bfloat16
TILE, WIDE, PIECES = 128, 256, 4


def send(x, to):
    return lax.ppermute(x, ALL, [(i, to(i) % 256) for i in range(256)])


def in_chip(x):
    return send(x, lambda i: i ^ 1)


def swap_even(x):
    return send(x, lambda i: i ^ 2)


def swap_odd(x):
    return send(x, lambda i: ((i + 2) ^ 2) - 2)


def dot(left, right):
    return jnp.dot(left, right, preferred_element_type=F32)


def dot_nt(left, right):
    return lax.dot_general(left, right, (((1,), (1,)), ((), ())), preferred_element_type=F32)


def to_row(column):
    return jnp.broadcast_to(column, (column.shape[0], 128)).T[:1]


def to_column(row):
    return jnp.broadcast_to(row, (128, row.shape[1])).T[:, :1]


def call(body, out, *arrays, scratch=(), flops=0, name=None, kept=()):
    vmem = pl.BlockSpec(memory_space=pltpu.VMEM)
    size = sum(a.size * a.dtype.itemsize for a in (*arrays, *out))
    return pl.pallas_call(
        body,
        out_shape=out,
        in_specs=[vmem] * len(arrays),
        out_specs=[vmem] * len(out),
        scratch_shapes=scratch,
        input_output_aliases=dict(kept),
        name=name,
        compiler_params=pltpu.CompilerParams(vmem_limit_bytes=16 * 2**20),
        cost_estimate=pl.CostEstimate(flops=flops, bytes_accessed=size, transcendentals=0),
    )(*arrays)


def embed(frames, head, offsets, emb, unit, rnorm, goal, goal_row, f, h, acc, sems):
    depth = head.shape[0]
    step = depth // PIECES
    copies = []
    for k in range(PIECES):
        cut = pl.ds(k * step, step)
        copies.append(pltpu.make_async_copy(frames.at[:, cut], f.at[:, cut], sems.at[0, k]))
        copies.append(pltpu.make_async_copy(head.at[cut, :], h.at[cut, :], sems.at[1, k]))
    for c in copies:
        c.start()
    row = offsets[...] + lax.broadcasted_iota(jnp.int32, offsets.shape, 1)
    goal_row[...] = row.astype(F32)
    goal[...] = to_column(row.astype(F32)).astype(jnp.int32)
    for k in range(PIECES):
        cut = pl.ds(k * step, step)
        copies[2 * k].wait()
        copies[2 * k + 1].wait()
        if k == 0:
            acc[...] = dot(f[:, cut], h[cut, :])
        elif k < PIECES - 1:
            acc[...] += dot(f[:, cut], h[cut, :])
    for r in range(0, acc.shape[0], WIDE):
        rows = pl.ds(r, WIDE)
        z = acc[rows, :] + dot(f[rows, cut], h[cut, :])
        norm = jnp.sqrt(jnp.sum(z * z, axis=1, keepdims=True) + 1e-06)
        inverse = 1.0 / norm
        u = z * inverse
        unit[rows, :] = u
        emb[rows, :] = u.astype(BF16)
        rnorm[rows, :] = inverse


def chip_sign():
    return 1 - 2 * lax.rem(lax.axis_index("x"), 2)


def crossed():
    return lax.rem(lax.axis_index("x") + lax.axis_index("core"), 2) == 1


def places():
    core = 1 - 2 * lax.axis_index("core")
    return (0, core, 2 * chip_sign(), -2 * chip_sign(), -core)


def pick(odd, even, token, out):
    out[...] = even[...]

    @pl.when(crossed())
    def _():
        out[...] = odd[...]


def score_tile(at, emb, block, goal, rows):
    score = SCALE * dot_nt(emb[rows, :], block[...])
    cols = lax.broadcasted_iota(jnp.int32, score.shape, 1) + at * block.shape[0]
    hit = cols == goal[rows, :]
    return score, jnp.sum(jnp.where(hit, score, 0.0), axis=1, keepdims=True)


def near(emb, peer, goal, unit, rnorm, e_all, total, pos, *kept):
    at = places()
    for r in range(0, emb.shape[0], WIDE):
        rows = pl.ds(r, WIDE)
        score, p0 = score_tile(0, emb, emb, goal, rows)
        e = jnp.exp(score)
        i = lax.broadcasted_iota(jnp.int32, e.shape, 0) + r
        e = jnp.where(i == lax.broadcasted_iota(jnp.int32, e.shape, 1), 0.0, e)
        e_all[0, rows, :] = e
        total[rows, :] = jnp.sum(e, axis=1, keepdims=True)
        score, p1 = score_tile(at[1], emb, peer, goal, rows)
        e = jnp.exp(score)
        e_all[1, rows, :] = e
        total[rows, :] += jnp.sum(e, axis=1, keepdims=True)
        pos[rows, :] = p0 + p1


def add_block(slot, emb, block, goal, e_all, total, pos):
    at = places()[slot]
    for r in range(0, emb.shape[0], WIDE):
        rows = pl.ds(r, WIDE)
        score, p = score_tile(at, emb, block, goal, rows)
        e = jnp.exp(score)
        e_all[slot, rows, :] = e
        total[rows, :] += jnp.sum(e, axis=1, keepdims=True)
        pos[rows, :] += p


def far(emb, even, odd, goal, e_in, total_in, pos_in, unit, rnorm, e_all, total, pos, *kept):
    add_block(2, emb, even, goal, e_all, total, pos)
    add_block(3, emb, odd, goal, e_all, total, pos)


def seal(
    emb, relay, goal, goal_row, e_in, total_in, pos_in, unit, rnorm,
    e_all, total, pos, unit_out, rnorm_out, inverse, note, losses,
):
    add_block(4, emb, relay, goal, e_all, total, pos)
    whole = to_row(total[...])
    inv = 1.0 / whole
    note[0:1, :] = inv
    note[1:2, :] = goal_row[...]
    inverse[...] = to_column(inv)
    losses[...] = jnp.log(whole) - to_row(pos[...])


def slope(e, at, goal, inverse, their_inverse, their_goal, rows):
    width = e.shape[1]
    i = lax.broadcasted_iota(jnp.int32, e.shape, 0) + rows.start
    j = lax.broadcasted_iota(jnp.int32, e.shape, 1) + at * width
    ours = (j == goal[rows, :]).astype(F32)
    theirs = (i == their_goal + at * width).astype(F32)
    return e * (inverse[rows, :] + their_inverse) - ours - theirs


def finish(
    goal, inverse, own_note, peer_note, odd_note, even_note, e_all, emb, peer, even, odd, relay, unit, rnorm,
    dz, g, acc,
):
    at = places()
    even_note, odd_note = even_note[...], odd_note[...]
    relay_note = jnp.where(crossed(), even_note, odd_note)[2:]
    notes = (own_note[...], peer_note[...], even_note[:2], odd_note[:2], relay_note)
    for k, (note, block) in enumerate(zip(notes, (emb, peer, even, odd, relay))):
        their_inverse, their_goal = note[0:1], note[1:2].astype(jnp.int32)
        for r in range(0, g.shape[1], TILE):
            rows = pl.ds(r, TILE)
            g[k % 2, rows, :] = slope(e_all[k, rows, :], at[k], goal, inverse, their_inverse, their_goal, rows).astype(BF16)
        if k == 0:
            acc[...] = dot(g[0], block[...])
        else:
            acc[...] += dot(g[k % 2], block[...])
    for r in range(0, emb.shape[0], TILE):
        rows = pl.ds(r, TILE)
        demb = SCALE * acc[rows, :]
        u = unit[rows, :]
        along = jnp.sum(u * demb, axis=1, keepdims=True)
        dz[rows, :] = ((demb - u * along) * rnorm[rows, :]).astype(BF16)


def turn(frames, token, mine, theirs):
    half, core = mine.shape[0], lax.axis_index("core")
    for out, k in ((mine, core), (theirs, 1 - core)):
        for c in range(0, half, 256):
            columns = pl.ds(pl.multiple_of(k * half + c, 128), 256)
            out[pl.ds(c, 256), :] = frames[:, columns].T


def add_up(got, out):
    total = got[0].astype(F32)
    for k in range(1, got.shape[0]):
        total += got[k].astype(F32)
    total = total.astype(BF16)
    for k in range(out.shape[0]):
        out[k] = total


def head_own(left, dz, out):
    out[...] = dot(left[...], dz[...])


def head_both(part, left, dz, out):
    cut = out.shape[2]
    for r in range(0, out.shape[1], WIDE):
        rows = pl.ds(r, WIDE)
        whole = (part[rows, :] + dot(left[rows, :], dz[...])).astype(BF16)
        for k in range(2):
            out[k, rows, :] = whole[:, k * cut : (k + 1) * cut]


def lay_out(other, part, *rest):
    out, sems = rest[-2:]
    core = lax.axis_index("core")
    _, size, cut = part.shape
    start = pl.multiple_of((1 - core if other else core) * size, size)
    copies = [
        pltpu.make_async_copy(part.at[k], out.at[pl.ds(start, size), pl.ds(k * cut, cut)], sems.at[k]) for k in range(2)
    ]
    for c in copies:
        c.start()
    for c in copies:
        c.wait()


def place_half(part, *whole):
    anywhere = pl.BlockSpec(memory_space=pl.ANY)
    return pl.pallas_call(
        functools.partial(lay_out, bool(whole)),
        out_shape=jax.ShapeDtypeStruct((2 * part.shape[1], 2 * part.shape[2]), part.dtype),
        in_specs=[anywhere] * (1 + len(whole)),
        out_specs=anywhere,
        scratch_shapes=[pltpu.SemaphoreType.DMA((2,))],
        input_output_aliases={1: 0} if whole else {},
        name="lay_out",
        compiler_params=pltpu.CompilerParams(vmem_limit_bytes=2**20),
    )(part, *whole)


def on_device(frames, head, offsets):
    rows, depth = frames.shape
    width = head.shape[1]
    shape = jax.ShapeDtypeStruct
    col, row = shape((rows, 1), F32), shape((1, rows), F32)
    square, tall = shape((rows, rows), F32), shape((rows, width), F32)
    note = shape((2, rows), F32)
    block_flops = 2 * rows * rows * width
    half = depth // 2
    vmem, hbm = pl.BlockSpec(memory_space=pltpu.VMEM), pl.BlockSpec(memory_space=pltpu.HBM)
    emb, unit, rnorm, goal, goal_row = pl.pallas_call(
        embed,
        in_specs=[hbm, hbm, vmem],
        out_specs=[vmem] * 5,
        out_shape=[shape((rows, width), BF16), tall, col, shape((rows, 1), jnp.int32), row],
        scratch_shapes=[
            pltpu.VMEM((rows, depth), BF16),
            pltpu.VMEM((depth, width), BF16),
            pltpu.VMEM((rows, width), F32),
            pltpu.SemaphoreType.DMA((2, PIECES)),
        ],
        name="embed",
        compiler_params=pltpu.CompilerParams(vmem_limit_bytes=51 * 2**20),
        cost_estimate=pl.CostEstimate(flops=2 * rows * depth * width, bytes_accessed=2**22, transcendentals=0),
    )(frames, head, offsets.reshape(1, rows))

    peer = in_chip(emb)
    odd = swap_odd(emb)
    even = swap_even(emb)
    everything = shape((5, rows, rows), F32)
    e_all, total, pos, unit, rnorm = call(
        near, [everything, col, col, tall, col], emb, peer, goal, unit, rnorm,
        kept=((3, 3), (4, 4)), flops=2 * block_flops, name="near",
    )
    mine, theirs = call(turn, [shape((half, rows), BF16)] * 2, frames, pos, name="turn")
    (shared,) = call(pick, [shape((rows, width), BF16)], odd, even, theirs, name="pick")
    relay = in_chip(shared)
    theirs = in_chip(theirs)
    e_all, total, pos, unit, rnorm = call(
        far, [everything, col, col, tall, col], emb, even, odd, goal, e_all, total, pos, unit, rnorm,
        kept=((4, 0), (5, 1), (6, 2), (7, 3), (8, 4)), flops=2 * block_flops, name="far",
    )
    e_all, total, pos, unit, rnorm, inverse, own_note, losses = call(
        seal, [everything, col, col, tall, col, col, note, row],
        emb, relay, goal, goal_row, e_all, total, pos, unit, rnorm,
        kept=((4, 0), (5, 1), (6, 2), (7, 3), (8, 4)), flops=block_flops, name="seal",
    )
    peer_note = in_chip(own_note)
    pair = jnp.concatenate([own_note, peer_note], axis=0)
    odd_note = swap_odd(pair)
    even_note = swap_even(pair)
    (dz,) = call(
        finish, [shape((rows, width), BF16)], goal, inverse, own_note, peer_note, odd_note, even_note, e_all,
        emb, peer, even, odd, relay, unit, rnorm,
        scratch=[pltpu.VMEM((2, rows, rows), BF16), pltpu.VMEM((rows, width), F32)],
        flops=5 * block_flops, name="finish",
    )
    dz_other = in_chip(dz)
    frame_grad = dot_nt(dz, head).astype(BF16)

    (partial,) = call(head_own, [shape((half, width), F32)], mine, dz, flops=2 * half * rows * width, name="head_own")
    (partial,) = call(
        head_both, [shape((2, half, width // 2), BF16)], partial, theirs, dz_other, flops=2 * half * rows * width, name="head_both"
    )
    share = (half // 16, width // 2)
    got = lax.all_to_all(partial.reshape(32, *share), NEAR, split_axis=0, concat_axis=0)
    (copies,) = call(add_up, [shape((4, *share), BF16)], got, name="add_near")
    got = lax.all_to_all(copies, "zh", split_axis=0, concat_axis=0)
    (copies,) = call(add_up, [shape((32, *share), BF16)], got, name="add_far")
    own = lax.all_to_all(copies, NEAR, split_axis=0, concat_axis=0).reshape(2, half, width // 2)
    other = in_chip(own)
    head_grad = place_half(other, place_half(own))
    return (losses.reshape(rows), frame_grad, head_grad)


def solution(mesh):
    torus = Mesh(mesh.devices.reshape(SIZES), ALL)
    return jax.shard_map(
        on_device,
        mesh=torus,
        in_specs=(P(ALL, None), P(), P(ALL)),
        out_specs=(P(ALL), P(ALL, None), P()),
        check_vma=False,
    )
```

```python
import functools

import jax
import jax.numpy as jnp
from jax import lax
from jax.experimental import pallas as pl
from jax.experimental.pallas import tpu as pltpu
from jax.sharding import Mesh, PartitionSpec as P

SCALE = 50.0
ALL = ("zh", "zl", "y", "x", "core")
SIZES = (4, 2, 4, 4, 2)
NEAR = ("zl", "y", "x")
F32, BF16 = jnp.float32, jnp.bfloat16
TILE, WIDE, PIECES = 128, 256, 2


def send(x, to):
    return lax.ppermute(x, ALL, [(i, to(i) % 256) for i in range(256)])


def in_chip(x):
    return send(x, lambda i: i ^ 1)


def swap_even(x):
    return send(x, lambda i: i ^ 2)


def swap_odd(x):
    return send(x, lambda i: ((i + 2) ^ 2) - 2)


def dot(left, right):
    return jnp.dot(left, right, preferred_element_type=F32)


def dot_nt(left, right):
    return lax.dot_general(left, right, (((1,), (1,)), ((), ())), preferred_element_type=F32)


def to_row(column):
    return jnp.broadcast_to(column, (column.shape[0], 128)).T[:1]


def to_column(row):
    return jnp.broadcast_to(row, (128, row.shape[1])).T[:, :1]


def call(body, out, *arrays, scratch=(), flops=0, name=None, kept=()):
    vmem = pl.BlockSpec(memory_space=pltpu.VMEM)
    size = sum(a.size * a.dtype.itemsize for a in (*arrays, *out))
    return pl.pallas_call(
        body,
        out_shape=out,
        in_specs=[vmem] * len(arrays),
        out_specs=[vmem] * len(out),
        scratch_shapes=scratch,
        input_output_aliases=dict(kept),
        name=name,
        compiler_params=pltpu.CompilerParams(vmem_limit_bytes=16 * 2**20),
        cost_estimate=pl.CostEstimate(flops=flops, bytes_accessed=size, transcendentals=0),
    )(*arrays)


def embed(frames, head, emb, unit, rnorm, f, h, acc, sems):
    depth = head.shape[0]
    step = depth // PIECES
    copies = []
    for k in range(PIECES):
        cut = pl.ds(k * step, step)
        copies.append(pltpu.make_async_copy(frames.at[:, cut], f.at[:, cut], sems.at[0, k]))
        copies.append(pltpu.make_async_copy(head.at[cut, :], h.at[cut, :], sems.at[1, k]))
    for c in copies:
        c.start()
    for k in range(PIECES):
        cut = pl.ds(k * step, step)
        copies[2 * k].wait()
        copies[2 * k + 1].wait()
        if k == 0:
            acc[...] = dot(f[:, cut], h[cut, :])
        elif k < PIECES - 1:
            acc[...] += dot(f[:, cut], h[cut, :])
    for r in range(0, acc.shape[0], WIDE):
        rows = pl.ds(r, WIDE)
        z = acc[rows, :] + dot(f[rows, cut], h[cut, :])
        norm = jnp.sqrt(jnp.sum(z * z, axis=1, keepdims=True) + 1e-06)
        inverse = 1.0 / norm
        u = z * inverse
        unit[rows, :] = u
        emb[rows, :] = u.astype(BF16)
        rnorm[rows, :] = inverse


def chip_sign():
    return 1 - 2 * lax.rem(lax.axis_index("x"), 2)


def crossed():
    return lax.rem(lax.axis_index("x") + lax.axis_index("core"), 2) == 1


def places():
    core = 1 - 2 * lax.axis_index("core")
    return (0, core, 2 * chip_sign(), -2 * chip_sign(), -core)


def pick(odd, even, token, out):
    out[...] = even[...]

    @pl.when(crossed())
    def _():
        out[...] = odd[...]


def score_tile(at, emb, block, goal, rows):
    score = SCALE * dot_nt(emb[rows, :], block[...])
    cols = lax.broadcasted_iota(jnp.int32, score.shape, 1) + at * block.shape[0]
    hit = cols == goal[rows, :]
    return score, jnp.sum(jnp.where(hit, score, 0.0), axis=1, keepdims=True)


def near(emb, peer, offsets, unit, rnorm, e_all, total, pos, unit_out, rnorm_out, goal, goal_row):
    at = places()
    positives = (offsets[...] + lax.broadcasted_iota(jnp.int32, offsets.shape, 1)).astype(F32)
    goal_row[...] = positives
    goal[...] = to_column(positives).astype(jnp.int32)
    for r in range(0, emb.shape[0], WIDE):
        rows = pl.ds(r, WIDE)
        score, p0 = score_tile(0, emb, emb, goal, rows)
        e = jnp.exp(score)
        i = lax.broadcasted_iota(jnp.int32, e.shape, 0) + r
        e = jnp.where(i == lax.broadcasted_iota(jnp.int32, e.shape, 1), 0.0, e)
        e_all[0, rows, :] = e
        total[rows, :] = jnp.sum(e, axis=1, keepdims=True)
        score, p1 = score_tile(at[1], emb, peer, goal, rows)
        e = jnp.exp(score)
        e_all[1, rows, :] = e
        total[rows, :] += jnp.sum(e, axis=1, keepdims=True)
        pos[rows, :] = p0 + p1


def add_block(slot, emb, block, goal, e_all, total, pos):
    at = places()[slot]
    for r in range(0, emb.shape[0], WIDE):
        rows = pl.ds(r, WIDE)
        score, p = score_tile(at, emb, block, goal, rows)
        e = jnp.exp(score)
        e_all[slot, rows, :] = e
        total[rows, :] += jnp.sum(e, axis=1, keepdims=True)
        pos[rows, :] += p


def far(emb, even, odd, goal, e_in, total_in, pos_in, unit, rnorm, e_all, total, pos, *kept):
    add_block(2, emb, even, goal, e_all, total, pos)
    add_block(3, emb, odd, goal, e_all, total, pos)


def seal(
    emb, relay, goal, goal_row, e_in, total_in, pos_in, unit, rnorm,
    e_all, total, pos, unit_out, rnorm_out, inverse, note,
):
    add_block(4, emb, relay, goal, e_all, total, pos)
    inverse[...] = 1.0 / total[...]
    note[0:1, :] = to_row(inverse[...])
    note[1:2, :] = goal_row[...]


def lose(total, pos, losses, token):
    losses[...] = to_row(jnp.log(total[...]) - pos[...])
    token[...] = jnp.zeros_like(token)


def slope(e, at, goal, inverse, their_inverse, their_goal, rows):
    width = e.shape[1]
    i = lax.broadcasted_iota(jnp.int32, e.shape, 0) + rows.start
    j = lax.broadcasted_iota(jnp.int32, e.shape, 1) + at * width
    ours = (j == goal[rows, :]).astype(F32)
    theirs = (i == their_goal + at * width).astype(F32)
    return e * (inverse[rows, :] + their_inverse) - ours - theirs


def finish(
    goal, inverse, own_note, peer_note, odd_note, even_note, e_all, emb, peer, even, odd, relay, unit, rnorm, token,
    dz, g, acc,
):
    at = places()
    even_note, odd_note = even_note[...], odd_note[...]
    relay_note = jnp.where(crossed(), even_note, odd_note)[2:]
    notes = (own_note[...], peer_note[...], even_note[:2], odd_note[:2], relay_note)
    for k, (note, block) in enumerate(zip(notes, (emb, peer, even, odd, relay))):
        their_inverse, their_goal = note[0:1], note[1:2].astype(jnp.int32)
        for r in range(0, g.shape[1], TILE):
            rows = pl.ds(r, TILE)
            g[k % 2, rows, :] = slope(e_all[k, rows, :], at[k], goal, inverse, their_inverse, their_goal, rows).astype(BF16)
        if k == 0:
            acc[...] = dot(g[0], block[...])
        else:
            acc[...] += dot(g[k % 2], block[...])
    for r in range(0, emb.shape[0], TILE):
        rows = pl.ds(r, TILE)
        demb = SCALE * acc[rows, :]
        u = unit[rows, :]
        along = jnp.sum(u * demb, axis=1, keepdims=True)
        dz[rows, :] = ((demb - u * along) * rnorm[rows, :]).astype(BF16)


def turn(frames, token, mine, theirs):
    half, core = mine.shape[0], lax.axis_index("core")
    for out, k in ((mine, core), (theirs, 1 - core)):
        for c in range(0, half, 256):
            columns = pl.ds(pl.multiple_of(k * half + c, 128), 256)
            out[pl.ds(c, 256), :] = frames[:, columns].T


def add_up(got, out):
    total = got[0].astype(F32)
    for k in range(1, got.shape[0]):
        total += got[k].astype(F32)
    total = total.astype(BF16)
    for k in range(out.shape[0]):
        out[k] = total


def head_own(left, dz, out):
    out[...] = dot(left[...], dz[...])


def head_both(part, left, dz, out):
    cut = out.shape[2]
    for r in range(0, out.shape[1], WIDE):
        rows = pl.ds(r, WIDE)
        whole = (part[rows, :] + dot(left[rows, :], dz[...])).astype(BF16)
        for k in range(2):
            out[k, rows, :] = whole[:, k * cut : (k + 1) * cut]


def half_copies(part, out, sems, core):
    _, size, cut = part.shape
    step = size // 2
    start = pl.multiple_of(core * size, size)
    return [
        pltpu.make_async_copy(
            part.at[k, pl.ds(r * step, step), :],
            out.at[pl.ds(start + r * step, step), pl.ds(k * cut, cut)],
            sems.at[k, r],
        )
        for k in range(2)
        for r in range(2)
    ]


def ends(dz, head, own, frame_grad, out, held, sems, out_sems):
    copies = half_copies(own, out, sems, lax.axis_index("core"))
    for c in copies:
        c.start()
    step = head.shape[0] // out_sems.shape[0]
    for k in range(out_sems.shape[0]):
        cut = pl.ds(k * step, step)
        held[:, cut] = dot_nt(dz[...], head[cut, :]).astype(BF16)
        copies.append(pltpu.make_async_copy(held.at[:, cut], frame_grad.at[:, cut], out_sems.at[k]))
        copies[-1].start()
    for c in copies:
        c.wait()


def last_half(other, whole, out, sems):
    copies = half_copies(other, out, sems, 1 - lax.axis_index("core"))
    for c in copies:
        c.start()
    for c in copies:
        c.wait()


def on_device(frames, head, offsets):
    rows, depth = frames.shape
    width = head.shape[1]
    shape = jax.ShapeDtypeStruct
    col, row = shape((rows, 1), F32), shape((1, rows), F32)
    square, tall = shape((rows, rows), F32), shape((rows, width), F32)
    note = shape((2, rows), F32)
    block_flops = 2 * rows * rows * width
    half = depth // 2
    vmem, hbm = pl.BlockSpec(memory_space=pltpu.VMEM), pl.BlockSpec(memory_space=pltpu.HBM)
    emb, unit, rnorm = pl.pallas_call(
        embed,
        in_specs=[hbm, hbm],
        out_specs=[vmem] * 3,
        out_shape=[shape((rows, width), BF16), tall, col],
        scratch_shapes=[
            pltpu.VMEM((rows, depth), BF16),
            pltpu.VMEM((depth, width), BF16),
            pltpu.VMEM((rows, width), F32),
            pltpu.SemaphoreType.DMA((2, PIECES)),
        ],
        name="embed",
        compiler_params=pltpu.CompilerParams(vmem_limit_bytes=51 * 2**20),
        cost_estimate=pl.CostEstimate(flops=2 * rows * depth * width, bytes_accessed=2**22, transcendentals=0),
    )(frames, head)

    peer = in_chip(emb)
    odd = swap_odd(emb)
    even = swap_even(emb)
    everything = shape((5, rows, rows), F32)
    e_all, total, pos, unit, rnorm, goal, goal_row = call(
        near, [everything, col, col, tall, col, shape((rows, 1), jnp.int32), row],
        emb, peer, offsets.reshape(1, rows), unit, rnorm,
        kept=((3, 3), (4, 4)), flops=2 * block_flops, name="near",
    )
    mine, theirs = call(turn, [shape((half, rows), BF16)] * 2, frames, pos, name="turn")
    (shared,) = call(pick, [shape((rows, width), BF16)], odd, even, theirs, name="pick")
    relay = in_chip(shared)
    theirs = in_chip(theirs)
    e_all, total, pos, unit, rnorm = call(
        far, [everything, col, col, tall, col], emb, even, odd, goal, e_all, total, pos, unit, rnorm,
        kept=((4, 0), (5, 1), (6, 2), (7, 3), (8, 4)), flops=2 * block_flops, name="far",
    )
    e_all, total, pos, unit, rnorm, inverse, own_note = call(
        seal, [everything, col, col, tall, col, col, note],
        emb, relay, goal, goal_row, e_all, total, pos, unit, rnorm,
        kept=((4, 0), (5, 1), (6, 2), (7, 3), (8, 4)), flops=block_flops, name="seal",
    )
    peer_note = in_chip(own_note)
    losses, token = call(lose, [row, shape((8, 128), F32)], total, pos, name="lose")
    pair = jnp.concatenate([own_note, peer_note], axis=0)
    odd_note = swap_odd(pair)
    even_note = swap_even(pair)
    (dz,) = call(
        finish, [shape((rows, width), BF16)], goal, inverse, own_note, peer_note, odd_note, even_note, e_all,
        emb, peer, even, odd, relay, unit, rnorm, token,
        scratch=[pltpu.VMEM((2, rows, rows), BF16), pltpu.VMEM((rows, width), F32)],
        flops=5 * block_flops, name="finish",
    )
    dz_other = in_chip(dz)

    (partial,) = call(head_own, [shape((half, width), F32)], mine, dz, flops=2 * half * rows * width, name="head_own")
    (partial,) = call(
        head_both, [shape((2, half, width // 2), BF16)], partial, theirs, dz_other, flops=2 * half * rows * width, name="head_both"
    )
    share = (half // 16, width // 2)
    got = lax.all_to_all(partial.reshape(32, *share), NEAR, split_axis=0, concat_axis=0)
    (copies,) = call(add_up, [shape((4, *share), BF16)], got, name="add_near")
    got = lax.all_to_all(copies, "zh", split_axis=0, concat_axis=0)
    (copies,) = call(add_up, [shape((32, *share), BF16)], got, name="add_far")
    own = lax.all_to_all(copies, NEAR, split_axis=0, concat_axis=0).reshape(2, half, width // 2)
    other = in_chip(own)
    anywhere = pl.BlockSpec(memory_space=pl.ANY)
    frame_grad, head_grad = pl.pallas_call(
        ends,
        in_specs=[vmem, vmem, anywhere],
        out_specs=[anywhere] * 2,
        out_shape=[shape((rows, depth), BF16), shape((depth, width), BF16)],
        scratch_shapes=[
            pltpu.VMEM((rows, depth), BF16), pltpu.SemaphoreType.DMA((2, 2)), pltpu.SemaphoreType.DMA((3,))
        ],
        name="ends",
        compiler_params=pltpu.CompilerParams(vmem_limit_bytes=16 * 2**20),
        cost_estimate=pl.CostEstimate(flops=2 * rows * depth * width, bytes_accessed=2**22, transcendentals=0),
    )(dz, head, own)
    head_grad = pl.pallas_call(
        last_half,
        in_specs=[anywhere] * 2,
        out_specs=anywhere,
        out_shape=shape((depth, width), BF16),
        scratch_shapes=[pltpu.SemaphoreType.DMA((2, 2))],
        input_output_aliases={1: 0},
        name="last_half",
        compiler_params=pltpu.CompilerParams(vmem_limit_bytes=2**20),
    )(other, head_grad)
    return (losses.reshape(rows), frame_grad, head_grad)


def solution(mesh):
    torus = Mesh(mesh.devices.reshape(SIZES), ALL)
    return jax.shard_map(
        on_device,
        mesh=torus,
        in_specs=(P(ALL, None), P(), P(ALL)),
        out_specs=(P(ALL), P(ALL, None), P()),
        check_vma=False,
    )
```

```python
import functools

import jax
import jax.numpy as jnp
from jax import lax
from jax.experimental import pallas as pl
from jax.experimental.pallas import tpu as pltpu
from jax.sharding import Mesh, PartitionSpec as P

SCALE = 50.0
ALL = ("zh", "zl", "y", "x", "core")
SIZES = (4, 2, 4, 4, 2)
NEAR = ("zl", "y", "x")
F32, BF16 = jnp.float32, jnp.bfloat16
TILE, WIDE = 128, 256


def send(x, to):
    return lax.ppermute(x, ALL, [(i, to(i) % 256) for i in range(256)])


def in_chip(x):
    return send(x, lambda i: i ^ 1)


def swap_even(x):
    return send(x, lambda i: i ^ 2)


def swap_odd(x):
    return send(x, lambda i: ((i + 2) ^ 2) - 2)


def dot(left, right):
    return jnp.dot(left, right, preferred_element_type=F32)


def dot_nt(left, right):
    return lax.dot_general(left, right, (((1,), (1,)), ((), ())), preferred_element_type=F32)


def to_row(column):
    return jnp.broadcast_to(column, (column.shape[0], 128)).T[:1]


def to_column(row):
    return jnp.broadcast_to(row, (128, row.shape[1])).T[:, :1]


def call(body, out, *arrays, scratch=(), flops=0, name=None, kept=()):
    vmem = pl.BlockSpec(memory_space=pltpu.VMEM)
    size = sum(a.size * a.dtype.itemsize for a in (*arrays, *out))
    return pl.pallas_call(
        body,
        out_shape=out,
        in_specs=[vmem] * len(arrays),
        out_specs=[vmem] * len(out),
        scratch_shapes=scratch,
        input_output_aliases=dict(kept),
        name=name,
        compiler_params=pltpu.CompilerParams(vmem_limit_bytes=16 * 2**20),
        cost_estimate=pl.CostEstimate(flops=flops, bytes_accessed=size, transcendentals=0),
    )(*arrays)


def embed(frames, head, emb, unit, rnorm, f, h, acc, sems):
    depth = head.shape[0]
    cuts = (pl.ds(0, 2 * depth // 3), pl.ds(2 * depth // 3, depth // 3))
    copies = []
    for k, cut in enumerate(cuts):
        copies.append(pltpu.make_async_copy(frames.at[:, cut], f.at[:, cut], sems.at[0, k]))
        copies.append(pltpu.make_async_copy(head.at[cut, :], h.at[cut, :], sems.at[1, k]))
    for c in copies:
        c.start()
    copies[0].wait()
    copies[1].wait()
    acc[...] = dot(f[:, cuts[0]], h[cuts[0], :])
    copies[2].wait()
    copies[3].wait()
    cut = cuts[1]
    for r in range(0, acc.shape[0], WIDE):
        rows = pl.ds(r, WIDE)
        z = acc[rows, :] + dot(f[rows, cut], h[cut, :])
        norm = jnp.sqrt(jnp.sum(z * z, axis=1, keepdims=True) + 1e-06)
        inverse = 1.0 / norm
        u = z * inverse
        unit[rows, :] = u
        emb[rows, :] = u.astype(BF16)
        rnorm[rows, :] = inverse


def chip_sign():
    return 1 - 2 * lax.rem(lax.axis_index("x"), 2)


def crossed():
    return lax.rem(lax.axis_index("x") + lax.axis_index("core"), 2) == 1


def places():
    core = 1 - 2 * lax.axis_index("core")
    return (0, core, 2 * chip_sign(), -2 * chip_sign(), -core)


def pick(even, odd, token, out):
    out[...] = even[...]

    @pl.when(crossed())
    def _():
        out[...] = odd[...]


def score_tile(at, emb, block, goal, rows):
    score = SCALE * dot_nt(emb[rows, :], block[...])
    cols = lax.broadcasted_iota(jnp.int32, score.shape, 1) + at * block.shape[0]
    hit = cols == goal[rows, :]
    return score, jnp.sum(jnp.where(hit, score, 0.0), axis=1, keepdims=True)


def near(emb, peer, offsets, unit, rnorm, e_all, total, pos, unit_out, rnorm_out, goal, goal_row):
    at = places()
    positives = (offsets[...] + lax.broadcasted_iota(jnp.int32, offsets.shape, 1)).astype(F32)
    goal_row[...] = positives
    goal[...] = to_column(positives).astype(jnp.int32)
    for r in range(0, emb.shape[0], WIDE):
        rows = pl.ds(r, WIDE)
        score, p0 = score_tile(0, emb, emb, goal, rows)
        e = jnp.exp(score)
        i = lax.broadcasted_iota(jnp.int32, e.shape, 0) + r
        e = jnp.where(i == lax.broadcasted_iota(jnp.int32, e.shape, 1), 0.0, e)
        e_all[0, rows, :] = e
        total[rows, :] = jnp.sum(e, axis=1, keepdims=True)
        score, p1 = score_tile(at[1], emb, peer, goal, rows)
        e = jnp.exp(score)
        e_all[1, rows, :] = e
        total[rows, :] += jnp.sum(e, axis=1, keepdims=True)
        pos[rows, :] = p0 + p1


def add_block(slot, emb, block, goal, e_all, total, pos):
    at = places()[slot]
    for r in range(0, emb.shape[0], WIDE):
        rows = pl.ds(r, WIDE)
        score, p = score_tile(at, emb, block, goal, rows)
        e = jnp.exp(score)
        e_all[slot, rows, :] = e
        total[rows, :] += jnp.sum(e, axis=1, keepdims=True)
        pos[rows, :] += p


def far(emb, even, odd, goal, e_in, total_in, pos_in, unit, rnorm, e_all, total, pos, *kept):
    add_block(2, emb, even, goal, e_all, total, pos)
    add_block(3, emb, odd, goal, e_all, total, pos)


def seal(
    emb, relay, goal, goal_row, e_in, total_in, pos_in, unit, rnorm,
    e_all, total, pos, unit_out, rnorm_out, inverse, note,
):
    add_block(4, emb, relay, goal, e_all, total, pos)
    inverse[...] = 1.0 / total[...]
    note[0:1, :] = to_row(inverse[...])
    note[1:2, :] = goal_row[...]


def lose(total, pos, losses, token):
    losses[...] = to_row(jnp.log(total[...]) - pos[...])
    token[...] = jnp.zeros_like(token)


def slope(e, inverse, their_inverse, left, right):
    weight = e * (inverse + their_inverse)
    return jnp.where(left == right, weight - 1.0, weight)


def finish(
    goal, inverse, own_note, peer_note, odd_note, even_note, e_all, emb, peer, even, odd, relay, unit, rnorm, token,
    dz, g, acc,
):
    at = places()
    even_note, odd_note = even_note[...], odd_note[...]
    relay_note = jnp.where(crossed(), even_note, odd_note)[2:]
    notes = (own_note[...], peer_note[...], even_note[:2], odd_note[:2], relay_note)
    size = g.shape[1]
    ids = lax.broadcasted_iota(jnp.int32, (1, size), 1)
    for k, (note, block) in enumerate(zip(notes, (emb, peer, even, odd, relay))):
        their_inverse, their_goal = note[0:1], note[1:2].astype(jnp.int32)
        shift = at[k] * size
        ahead = at[k] >= 0
        right = jnp.where(ahead, ids + shift, their_goal + shift)
        for r in range(0, size, TILE):
            rows = pl.ds(r, TILE)
            mine = lax.broadcasted_iota(jnp.int32, (TILE, 1), 0) + r
            left = jnp.where(ahead, goal[rows, :], mine)
            weight = slope(e_all[k, rows, :], inverse[rows, :], their_inverse, left, right)
            if k == 0:
                weight = jnp.where(mine == their_goal, weight - 1.0, weight)
            g[k % 2, rows, :] = weight.astype(BF16)
        if k == 0:
            acc[...] = dot(g[0], block[...])
        else:
            acc[...] += dot(g[k % 2], block[...])
    for r in range(0, emb.shape[0], TILE):
        rows = pl.ds(r, TILE)
        demb = SCALE * acc[rows, :]
        u = unit[rows, :]
        along = jnp.sum(u * demb, axis=1, keepdims=True)
        dz[rows, :] = ((demb - u * along) * rnorm[rows, :]).astype(BF16)


def turn(frames, token, mine, theirs):
    half, core = mine.shape[0], lax.axis_index("core")
    for out, k in ((mine, core), (theirs, 1 - core)):
        for c in range(0, half, 256):
            columns = pl.ds(pl.multiple_of(k * half + c, 128), 256)
            out[pl.ds(c, 256), :] = frames[:, columns].T


def add_up(got, out):
    total = got[0].astype(F32)
    for k in range(1, got.shape[0]):
        total += got[k].astype(F32)
    total = total.astype(BF16)
    for k in range(out.shape[0]):
        out[k] = total


def head_own(left, dz, out):
    out[...] = dot(left[...], dz[...])


def head_both(part, left, dz, out):
    cut = out.shape[2]
    for r in range(0, out.shape[1], WIDE):
        rows = pl.ds(r, WIDE)
        whole = (part[rows, :] + dot(left[rows, :], dz[...])).astype(BF16)
        for k in range(2):
            out[k, rows, :] = whole[:, k * cut : (k + 1) * cut]


def half_copies(part, out, sems, core):
    _, size, cut = part.shape
    step = size // 2
    start = pl.multiple_of(core * size, size)
    return [
        pltpu.make_async_copy(
            part.at[k, pl.ds(r * step, step), :],
            out.at[pl.ds(start + r * step, step), pl.ds(k * cut, cut)],
            sems.at[k, r],
        )
        for k in range(2)
        for r in range(2)
    ]


def ends(dz, head, own, frame_grad, out, held, sems, out_sems):
    copies = half_copies(own, out, sems, lax.axis_index("core"))
    for c in copies:
        c.start()
    step = head.shape[0] // out_sems.shape[0]
    for k in range(out_sems.shape[0]):
        cut = pl.ds(k * step, step)
        held[:, cut] = dot_nt(dz[...], head[cut, :]).astype(BF16)
        copies.append(pltpu.make_async_copy(held.at[:, cut], frame_grad.at[:, cut], out_sems.at[k]))
        copies[-1].start()
    for c in copies:
        c.wait()


def last_half(other, whole, out, sems):
    copies = half_copies(other, out, sems, 1 - lax.axis_index("core"))
    for c in copies:
        c.start()
    for c in copies:
        c.wait()


def on_device(frames, head, offsets):
    rows, depth = frames.shape
    width = head.shape[1]
    shape = jax.ShapeDtypeStruct
    col, row = shape((rows, 1), F32), shape((1, rows), F32)
    square, tall = shape((rows, rows), F32), shape((rows, width), F32)
    note = shape((2, rows), F32)
    block_flops = 2 * rows * rows * width
    half = depth // 2
    vmem, hbm = pl.BlockSpec(memory_space=pltpu.VMEM), pl.BlockSpec(memory_space=pltpu.HBM)
    emb, unit, rnorm = pl.pallas_call(
        embed,
        in_specs=[hbm, hbm],
        out_specs=[vmem] * 3,
        out_shape=[shape((rows, width), BF16), tall, col],
        scratch_shapes=[
            pltpu.VMEM((rows, depth), BF16),
            pltpu.VMEM((depth, width), BF16),
            pltpu.VMEM((rows, width), F32),
            pltpu.SemaphoreType.DMA((2, 2)),
        ],
        name="embed",
        compiler_params=pltpu.CompilerParams(vmem_limit_bytes=51 * 2**20),
        cost_estimate=pl.CostEstimate(flops=2 * rows * depth * width, bytes_accessed=2**22, transcendentals=0),
    )(frames, head)

    peer = in_chip(emb)
    odd = swap_odd(emb)
    even = swap_even(emb)
    everything = shape((5, rows, rows), F32)
    e_all, total, pos, unit, rnorm, goal, goal_row = call(
        near, [everything, col, col, tall, col, shape((rows, 1), jnp.int32), row],
        emb, peer, offsets.reshape(1, rows), unit, rnorm,
        kept=((3, 3), (4, 4)), flops=2 * block_flops, name="near",
    )
    mine, theirs = call(turn, [shape((half, rows), BF16)] * 2, frames, pos, name="turn")
    (shared,) = call(pick, [shape((rows, width), BF16)], even, odd, theirs, name="pick")
    relay = in_chip(shared)
    theirs = in_chip(theirs)
    e_all, total, pos, unit, rnorm = call(
        far, [everything, col, col, tall, col], emb, even, odd, goal, e_all, total, pos, unit, rnorm,
        kept=((4, 0), (5, 1), (6, 2), (7, 3), (8, 4)), flops=2 * block_flops, name="far",
    )
    e_all, total, pos, unit, rnorm, inverse, own_note = call(
        seal, [everything, col, col, tall, col, col, note],
        emb, relay, goal, goal_row, e_all, total, pos, unit, rnorm,
        kept=((4, 0), (5, 1), (6, 2), (7, 3), (8, 4)), flops=block_flops, name="seal",
    )
    peer_note = in_chip(own_note)
    losses, token = call(lose, [row, shape((8, 128), F32)], total, pos, name="lose")
    pair = jnp.concatenate([own_note, peer_note], axis=0)
    odd_note = swap_odd(pair)
    even_note = swap_even(pair)
    (dz,) = call(
        finish, [shape((rows, width), BF16)], goal, inverse, own_note, peer_note, odd_note, even_note, e_all,
        emb, peer, even, odd, relay, unit, rnorm, token,
        scratch=[pltpu.VMEM((2, rows, rows), BF16), pltpu.VMEM((rows, width), F32)],
        flops=5 * block_flops, name="finish",
    )
    dz_other = in_chip(dz)

    (partial,) = call(head_own, [shape((half, width), F32)], mine, dz, flops=2 * half * rows * width, name="head_own")
    (partial,) = call(
        head_both, [shape((2, half, width // 2), BF16)], partial, theirs, dz_other, flops=2 * half * rows * width, name="head_both"
    )
    share = (half // 16, width // 2)
    got = lax.all_to_all(partial.reshape(32, *share), NEAR, split_axis=0, concat_axis=0)
    (copies,) = call(add_up, [shape((4, *share), BF16)], got, name="add_near")
    got = lax.all_to_all(copies, "zh", split_axis=0, concat_axis=0)
    (copies,) = call(add_up, [shape((32, *share), BF16)], got, name="add_far")
    own = lax.all_to_all(copies, NEAR, split_axis=0, concat_axis=0).reshape(2, half, width // 2)
    other = in_chip(own)
    anywhere = pl.BlockSpec(memory_space=pl.ANY)
    frame_grad, head_grad = pl.pallas_call(
        ends,
        in_specs=[vmem, vmem, anywhere],
        out_specs=[anywhere] * 2,
        out_shape=[shape((rows, depth), BF16), shape((depth, width), BF16)],
        scratch_shapes=[
            pltpu.VMEM((rows, depth), BF16), pltpu.SemaphoreType.DMA((2, 2)), pltpu.SemaphoreType.DMA((3,))
        ],
        name="ends",
        compiler_params=pltpu.CompilerParams(vmem_limit_bytes=16 * 2**20),
        cost_estimate=pl.CostEstimate(flops=2 * rows * depth * width, bytes_accessed=2**22, transcendentals=0),
    )(dz, head, own)
    head_grad = pl.pallas_call(
        last_half,
        in_specs=[anywhere] * 2,
        out_specs=anywhere,
        out_shape=shape((depth, width), BF16),
        scratch_shapes=[pltpu.SemaphoreType.DMA((2, 2))],
        input_output_aliases={1: 0},
        name="last_half",
        compiler_params=pltpu.CompilerParams(vmem_limit_bytes=2**20),
    )(other, head_grad)
    return (losses.reshape(rows), frame_grad, head_grad)


def solution(mesh):
    torus = Mesh(mesh.devices.reshape(SIZES), ALL)
    return jax.shard_map(
        on_device,
        mesh=torus,
        in_specs=(P(ALL, None), P(), P(ALL)),
        out_specs=(P(ALL), P(ALL, None), P()),
        check_vma=False,
    )
```

```python
import functools

import jax
import jax.numpy as jnp
from jax import lax
from jax.experimental import pallas as pl
from jax.experimental.pallas import tpu as pltpu
from jax.sharding import Mesh, PartitionSpec as P

SCALE = 50.0
ALL = ("zh", "zl", "y", "x", "core")
SIZES = (4, 2, 4, 4, 2)
NEAR = ("zl", "y", "x")
F32, BF16 = jnp.float32, jnp.bfloat16
TILE, WIDE = 128, 256


def send(x, to):
    return lax.ppermute(x, ALL, [(i, to(i) % 256) for i in range(256)])


def in_chip(x):
    return send(x, lambda i: i ^ 1)


def swap_even(x):
    return send(x, lambda i: i ^ 2)


def swap_odd(x):
    return send(x, lambda i: ((i + 2) ^ 2) - 2)


def dot(left, right):
    return jnp.dot(left, right, preferred_element_type=F32)


def dot_nt(left, right):
    return lax.dot_general(left, right, (((1,), (1,)), ((), ())), preferred_element_type=F32)


def to_row(column):
    return jnp.broadcast_to(column, (column.shape[0], 128)).T[:1]


def to_column(row):
    return jnp.broadcast_to(row, (128, row.shape[1])).T[:, :1]


def call(body, out, *arrays, scratch=(), flops=0, name=None, kept=()):
    vmem = pl.BlockSpec(memory_space=pltpu.VMEM)
    size = sum(a.size * a.dtype.itemsize for a in (*arrays, *out))
    return pl.pallas_call(
        body,
        out_shape=out,
        in_specs=[vmem] * len(arrays),
        out_specs=[vmem] * len(out),
        scratch_shapes=scratch,
        input_output_aliases=dict(kept),
        name=name,
        compiler_params=pltpu.CompilerParams(vmem_limit_bytes=16 * 2**20),
        cost_estimate=pl.CostEstimate(flops=flops, bytes_accessed=size, transcendentals=0),
    )(*arrays)


def embed(frames, head, emb, unit, rnorm, f, h, acc, sems):
    depth = head.shape[0]
    cuts = (pl.ds(0, depth // 2), pl.ds(depth // 2, depth // 2))
    copies = []
    for k, cut in enumerate(cuts):
        copies.append(pltpu.make_async_copy(frames.at[:, cut], f.at[:, cut], sems.at[0, k]))
        copies.append(pltpu.make_async_copy(head.at[cut, :], h.at[cut, :], sems.at[1, k]))
    for c in copies:
        c.start()
    copies[0].wait()
    copies[1].wait()
    acc[...] = dot(f[:, cuts[0]], h[cuts[0], :])
    copies[2].wait()
    copies[3].wait()
    cut = cuts[1]
    for r in range(0, acc.shape[0], WIDE):
        rows = pl.ds(r, WIDE)
        z = acc[rows, :] + dot(f[rows, cut], h[cut, :])
        norm = jnp.sqrt(jnp.sum(z * z, axis=1, keepdims=True) + 1e-06)
        inverse = 1.0 / norm
        u = z * inverse
        unit[rows, :] = u
        emb[rows, :] = u.astype(BF16)
        rnorm[rows, :] = inverse


def chip_sign():
    return 1 - 2 * lax.rem(lax.axis_index("x"), 2)


def crossed():
    return lax.rem(lax.axis_index("x") + lax.axis_index("core"), 2) == 1


def places():
    core = 1 - 2 * lax.axis_index("core")
    return (0, core, 2 * chip_sign(), -2 * chip_sign(), -core)


def pick(even, odd, token, out):
    out[...] = even[...]

    @pl.when(crossed())
    def _():
        out[...] = odd[...]


def score_tile(at, emb, block, goal, rows):
    score = SCALE * dot_nt(emb[rows, :], block[...])
    cols = lax.broadcasted_iota(jnp.int32, score.shape, 1) + at * block.shape[0]
    hit = cols == goal[rows, :]
    return score, jnp.sum(jnp.where(hit, score, 0.0), axis=1, keepdims=True)


def near(emb, peer, offsets, unit, rnorm, e_all, total, pos, unit_out, rnorm_out, goal, goal_row):
    at = places()
    positives = (offsets[...] + lax.broadcasted_iota(jnp.int32, offsets.shape, 1)).astype(F32)
    goal_row[...] = positives
    goal[...] = to_column(positives).astype(jnp.int32)
    for r in range(0, emb.shape[0], WIDE):
        rows = pl.ds(r, WIDE)
        score, p0 = score_tile(0, emb, emb, goal, rows)
        e = jnp.exp(score)
        i = lax.broadcasted_iota(jnp.int32, e.shape, 0) + r
        e = jnp.where(i == lax.broadcasted_iota(jnp.int32, e.shape, 1), 0.0, e)
        e_all[0, rows, :] = e
        total[rows, :] = jnp.sum(e, axis=1, keepdims=True)
        score, p1 = score_tile(at[1], emb, peer, goal, rows)
        e = jnp.exp(score)
        e_all[1, rows, :] = e
        total[rows, :] += jnp.sum(e, axis=1, keepdims=True)
        pos[rows, :] = p0 + p1


def add_block(slot, emb, block, goal, e_all, total, pos):
    at = places()[slot]
    for r in range(0, emb.shape[0], WIDE):
        rows = pl.ds(r, WIDE)
        score, p = score_tile(at, emb, block, goal, rows)
        e = jnp.exp(score)
        e_all[slot, rows, :] = e
        total[rows, :] += jnp.sum(e, axis=1, keepdims=True)
        pos[rows, :] += p


def far(
    emb, even, odd, peer, goal, goal_row, token, e_in, total_in, pos_in, unit, rnorm,
    e_all, total, pos, unit_out, rnorm_out, note, part,
):
    def for_peer(block):
        for r in range(0, peer.shape[0], WIDE):
            rows = pl.ds(r, WIDE)
            e = jnp.exp(SCALE * dot_nt(peer[rows, :], block[...]))
            part[rows, :] = jnp.sum(e, axis=1, keepdims=True)

    pl.when(crossed())(lambda: for_peer(odd))
    pl.when(jnp.logical_not(crossed()))(lambda: for_peer(even))
    add_block(2, emb, even, goal, e_all, total, pos)
    add_block(3, emb, odd, goal, e_all, total, pos)
    note[0:1, :] = to_row(total[...])
    note[1:2, :] = to_row(part[...])
    note[2:3, :] = goal_row[...]
    note[3:4, :] = jnp.zeros_like(goal_row)


def combine(own, peer, pair, inverse):
    inv = 1.0 / (own[0:1, :] + peer[1:2, :])
    inverse[...] = to_column(inv)
    pair[0:1, :] = inv
    pair[1:2, :] = own[2:3, :]
    pair[2:3, :] = 1.0 / (peer[0:1, :] + own[1:2, :])
    pair[3:4, :] = peer[2:3, :]


def seal(emb, relay, goal, e_in, total_in, pos_in, unit, rnorm, e_all, total, pos, *kept):
    add_block(4, emb, relay, goal, e_all, total, pos)


def lose(total, pos, losses, token):
    losses[...] = to_row(jnp.log(total[...]) - pos[...])
    token[...] = jnp.zeros_like(token)


def slope(e, inverse, their_inverse, left, right):
    weight = e * (inverse + their_inverse)
    return jnp.where(left == right, weight - 1.0, weight)


def finish(
    goal, inverse, pair, even_note, odd_note, e_all, emb, peer, even, odd, relay, unit, rnorm, token,
    dz, g, acc,
):
    at = places()
    pair, even_note, odd_note = pair[...], even_note[...], odd_note[...]
    relay_note = jnp.where(crossed(), even_note, odd_note)[2:]
    notes = (pair[:2], pair[2:], even_note[:2], odd_note[:2], relay_note)
    blocks = (emb, peer, even, odd, relay)
    size = g.shape[1]
    ids = lax.broadcasted_iota(jnp.int32, (1, size), 1)

    def slopes(k, rows):
        note = notes[k]
        their_inverse, their_goal = note[0:1], note[1:2].astype(jnp.int32)
        shift = at[k] * size
        ahead = at[k] >= 0
        right = jnp.where(ahead, ids + shift, their_goal + shift)
        mine = lax.broadcasted_iota(jnp.int32, (rows.size, 1), 0) + rows.start
        left = jnp.where(ahead, goal[rows, :], mine)
        weight = slope(e_all[k, rows, :], inverse[rows, :], their_inverse, left, right)
        if k == 0:
            weight = jnp.where(mine == their_goal, weight - 1.0, weight)
        g[k % 2, rows, :] = weight.astype(BF16)

    tiles = [pl.ds(r, WIDE) for r in range(0, size, WIDE)]
    for rows in tiles:
        slopes(0, rows)
    for k, block in enumerate(blocks):
        for rows in tiles:
            product = dot(g[k % 2, rows, :], block[...])
            if k + 1 < len(blocks):
                slopes(k + 1, rows)
            if k == 0:
                acc[rows, :] = product
            else:
                acc[rows, :] += product
    for r in range(0, emb.shape[0], TILE):
        rows = pl.ds(r, TILE)
        demb = SCALE * acc[rows, :]
        u = unit[rows, :]
        along = jnp.sum(u * demb, axis=1, keepdims=True)
        dz[rows, :] = ((demb - u * along) * rnorm[rows, :]).astype(BF16)


def turn(frames, token, mine, theirs):
    half, core = mine.shape[0], lax.axis_index("core")
    for out, k in ((mine, core), (theirs, 1 - core)):
        for c in range(0, half, 256):
            columns = pl.ds(pl.multiple_of(k * half + c, 128), 256)
            out[pl.ds(c, 256), :] = frames[:, columns].T


def add_up(got, out):
    total = got[0].astype(F32)
    for k in range(1, got.shape[0]):
        total += got[k].astype(F32)
    total = total.astype(BF16)
    for k in range(out.shape[0]):
        out[k] = total


def head_own(left, dz, out):
    out[...] = dot(left[...], dz[...])


def head_both(part, left, dz, out):
    cut = out.shape[2]
    for r in range(0, out.shape[1], WIDE):
        rows = pl.ds(r, WIDE)
        whole = (part[rows, :] + dot(left[rows, :], dz[...])).astype(BF16)
        for k in range(2):
            out[k, rows, :] = whole[:, k * cut : (k + 1) * cut]


def half_copies(part, out, sems, core):
    _, size, cut = part.shape
    step = size // 2
    start = pl.multiple_of(core * size, size)
    return [
        pltpu.make_async_copy(
            part.at[k, pl.ds(r * step, step), :],
            out.at[pl.ds(start + r * step, step), pl.ds(k * cut, cut)],
            sems.at[k, r],
        )
        for k in range(2)
        for r in range(2)
    ]


def ends(dz, head, own, frame_grad, out, held, sems, out_sems):
    copies = half_copies(own, out, sems, lax.axis_index("core"))
    for c in copies:
        c.start()
    step = head.shape[0] // out_sems.shape[0]
    for k in range(out_sems.shape[0]):
        cut = pl.ds(k * step, step)
        held[:, cut] = dot_nt(dz[...], head[cut, :]).astype(BF16)
        copies.append(pltpu.make_async_copy(held.at[:, cut], frame_grad.at[:, cut], out_sems.at[k]))
        copies[-1].start()
    for c in copies:
        c.wait()


def last_half(other, whole, out, sems):
    copies = half_copies(other, out, sems, 1 - lax.axis_index("core"))
    for c in copies:
        c.start()
    for c in copies:
        c.wait()


def on_device(frames, head, offsets):
    rows, depth = frames.shape
    width = head.shape[1]
    shape = jax.ShapeDtypeStruct
    col, row = shape((rows, 1), F32), shape((1, rows), F32)
    square, tall = shape((rows, rows), F32), shape((rows, width), F32)
    note = shape((2, rows), F32)
    block_flops = 2 * rows * rows * width
    half = depth // 2
    vmem, hbm = pl.BlockSpec(memory_space=pltpu.VMEM), pl.BlockSpec(memory_space=pltpu.HBM)
    emb, unit, rnorm = pl.pallas_call(
        embed,
        in_specs=[hbm, hbm],
        out_specs=[vmem] * 3,
        out_shape=[shape((rows, width), BF16), tall, col],
        scratch_shapes=[
            pltpu.VMEM((rows, depth), BF16),
            pltpu.VMEM((depth, width), BF16),
            pltpu.VMEM((rows, width), F32),
            pltpu.SemaphoreType.DMA((2, 2)),
        ],
        name="embed",
        compiler_params=pltpu.CompilerParams(vmem_limit_bytes=51 * 2**20),
        cost_estimate=pl.CostEstimate(flops=2 * rows * depth * width, bytes_accessed=2**22, transcendentals=0),
    )(frames, head)

    peer = in_chip(emb)
    odd = swap_odd(emb)
    even = swap_even(emb)
    everything = shape((5, rows, rows), F32)
    e_all, total, pos, unit, rnorm, goal, goal_row = call(
        near, [everything, col, col, tall, col, shape((rows, 1), jnp.int32), row],
        emb, peer, offsets.reshape(1, rows), unit, rnorm,
        kept=((3, 3), (4, 4)), flops=2 * block_flops, name="near",
    )
    mine, theirs = call(turn, [shape((half, rows), BF16)] * 2, frames, pos, name="turn")
    theirs = in_chip(theirs)
    state, keep = [everything, col, col, tall, col], lambda k: tuple((k + j, j) for j in range(5))
    note = shape((4, rows), F32)
    e_all, total, pos, unit, rnorm, own_note = call(
        far, state + [note], emb, even, odd, peer, goal, goal_row, theirs, e_all, total, pos, unit, rnorm,
        kept=keep(7), scratch=[pltpu.VMEM((rows, 1), F32)], flops=3 * block_flops, name="far",
    )
    peer_note = in_chip(own_note)
    pair, inverse = call(combine, [note, col], own_note, peer_note, name="combine")
    odd_note = swap_odd(pair)
    even_note = swap_even(pair)
    (shared,) = call(pick, [shape((rows, width), BF16)], even, odd, pair, name="pick")
    relay = in_chip(shared)
    e_all, total, pos, unit, rnorm = call(
        seal, state, emb, relay, goal, e_all, total, pos, unit, rnorm, kept=keep(3), flops=block_flops, name="seal",
    )
    losses, token = call(lose, [row, shape((8, 128), F32)], total, pos, name="lose")
    (dz,) = call(
        finish, [shape((rows, width), BF16)], goal, inverse, pair, even_note, odd_note, e_all,
        emb, peer, even, odd, relay, unit, rnorm, token,
        scratch=[pltpu.VMEM((2, rows, rows), BF16), pltpu.VMEM((rows, width), F32)],
        flops=5 * block_flops, name="finish",
    )
    dz_other = in_chip(dz)

    (partial,) = call(head_own, [shape((half, width), F32)], mine, dz, flops=2 * half * rows * width, name="head_own")
    (partial,) = call(
        head_both, [shape((2, half, width // 2), BF16)], partial, theirs, dz_other, flops=2 * half * rows * width, name="head_both"
    )
    share = (half // 16, width // 2)
    got = lax.all_to_all(partial.reshape(32, *share), NEAR, split_axis=0, concat_axis=0)
    (copies,) = call(add_up, [shape((4, *share), BF16)], got, name="add_near")
    got = lax.all_to_all(copies, "zh", split_axis=0, concat_axis=0)
    (copies,) = call(add_up, [shape((32, *share), BF16)], got, name="add_far")
    own = lax.all_to_all(copies, NEAR, split_axis=0, concat_axis=0).reshape(2, half, width // 2)
    other = in_chip(own)
    anywhere = pl.BlockSpec(memory_space=pl.ANY)
    frame_grad, head_grad = pl.pallas_call(
        ends,
        in_specs=[vmem, vmem, anywhere],
        out_specs=[anywhere] * 2,
        out_shape=[shape((rows, depth), BF16), shape((depth, width), BF16)],
        scratch_shapes=[
            pltpu.VMEM((rows, depth), BF16), pltpu.SemaphoreType.DMA((2, 2)), pltpu.SemaphoreType.DMA((3,))
        ],
        name="ends",
        compiler_params=pltpu.CompilerParams(vmem_limit_bytes=16 * 2**20),
        cost_estimate=pl.CostEstimate(flops=2 * rows * depth * width, bytes_accessed=2**22, transcendentals=0),
    )(dz, head, own)
    head_grad = pl.pallas_call(
        last_half,
        in_specs=[anywhere] * 2,
        out_specs=anywhere,
        out_shape=shape((depth, width), BF16),
        scratch_shapes=[pltpu.SemaphoreType.DMA((2, 2))],
        input_output_aliases={1: 0},
        name="last_half",
        compiler_params=pltpu.CompilerParams(vmem_limit_bytes=2**20),
    )(other, head_grad)
    return (losses.reshape(rows), frame_grad, head_grad)


def solution(mesh):
    torus = Mesh(mesh.devices.reshape(SIZES), ALL)
    return jax.shard_map(
        on_device,
        mesh=torus,
        in_specs=(P(ALL, None), P(), P(ALL)),
        out_specs=(P(ALL), P(ALL, None), P()),
        check_vma=False,
    )
```

```python
import functools

import jax
import jax.numpy as jnp
from jax import lax
from jax.experimental import pallas as pl
from jax.experimental.pallas import tpu as pltpu
from jax.sharding import Mesh, PartitionSpec as P

SCALE = 50.0
ALL = ("zh", "zl", "y", "x", "core")
SIZES = (4, 2, 4, 4, 2)
NEAR = ("zl", "y", "x")
F32, BF16 = jnp.float32, jnp.bfloat16
TILE, WIDE = 128, 256


def send(x, to):
    return lax.ppermute(x, ALL, [(i, to(i) % 256) for i in range(256)])


def in_chip(x):
    return send(x, lambda i: i ^ 1)


def swap_even(x):
    return send(x, lambda i: i ^ 2)


def swap_odd(x):
    return send(x, lambda i: ((i + 2) ^ 2) - 2)


def dot(left, right):
    return jnp.dot(left, right, preferred_element_type=F32)


def dot_nt(left, right):
    return lax.dot_general(left, right, (((1,), (1,)), ((), ())), preferred_element_type=F32)


def to_row(column):
    return jnp.broadcast_to(column, (column.shape[0], 128)).T[:1]


def to_column(row):
    return jnp.broadcast_to(row, (128, row.shape[1])).T[:, :1]


def call(body, out, *arrays, scratch=(), flops=0, name=None, kept=()):
    vmem = pl.BlockSpec(memory_space=pltpu.VMEM)
    size = sum(a.size * a.dtype.itemsize for a in (*arrays, *out))
    return pl.pallas_call(
        body,
        out_shape=out,
        in_specs=[vmem] * len(arrays),
        out_specs=[vmem] * len(out),
        scratch_shapes=scratch,
        input_output_aliases=dict(kept),
        name=name,
        compiler_params=pltpu.CompilerParams(vmem_limit_bytes=16 * 2**20),
        cost_estimate=pl.CostEstimate(flops=flops, bytes_accessed=size, transcendentals=0),
    )(*arrays)


def embed(frames, head, emb, unit, rnorm, f, h, acc, sems):
    depth = head.shape[0]
    cuts = (pl.ds(0, depth // 2), pl.ds(depth // 2, depth // 2))
    copies = []
    for k, cut in enumerate(cuts):
        copies.append(pltpu.make_async_copy(frames.at[:, cut], f.at[:, cut], sems.at[0, k]))
        copies.append(pltpu.make_async_copy(head.at[cut, :], h.at[cut, :], sems.at[1, k]))
    for c in copies:
        c.start()
    copies[0].wait()
    copies[1].wait()
    acc[...] = dot(f[:, cuts[0]], h[cuts[0], :])
    copies[2].wait()
    copies[3].wait()
    cut = cuts[1]
    for r in range(0, acc.shape[0], WIDE):
        rows = pl.ds(r, WIDE)
        z = acc[rows, :] + dot(f[rows, cut], h[cut, :])
        norm = jnp.sqrt(jnp.sum(z * z, axis=1, keepdims=True) + 1e-06)
        inverse = 1.0 / norm
        u = z * inverse
        unit[rows, :] = u
        emb[rows, :] = u.astype(BF16)
        rnorm[rows, :] = inverse


def chip_sign():
    return 1 - 2 * lax.rem(lax.axis_index("x"), 2)


def crossed():
    return lax.rem(lax.axis_index("x") + lax.axis_index("core"), 2) == 1


def places():
    core = 1 - 2 * lax.axis_index("core")
    return (0, core, 2 * chip_sign(), -2 * chip_sign(), -core)


def pick(even, odd, token, out):
    out[...] = even[...]

    @pl.when(crossed())
    def _():
        out[...] = odd[...]


def score_tile(at, emb, block, goal, rows):
    score = SCALE * dot_nt(emb[rows, :], block[...])
    cols = lax.broadcasted_iota(jnp.int32, score.shape, 1) + at * block.shape[0]
    hit = cols == goal[rows, :]
    return score, jnp.sum(jnp.where(hit, score, 0.0), axis=1, keepdims=True)


def near(emb, peer, offsets, unit, rnorm, e_all, total, pos, unit_out, rnorm_out, goal, goal_row):
    at = places()
    positives = (offsets[...] + lax.broadcasted_iota(jnp.int32, offsets.shape, 1)).astype(F32)
    goal_row[...] = positives
    goal[...] = to_column(positives).astype(jnp.int32)
    for r in range(0, emb.shape[0], WIDE):
        rows = pl.ds(r, WIDE)
        score, p0 = score_tile(0, emb, emb, goal, rows)
        e = jnp.exp(score)
        i = lax.broadcasted_iota(jnp.int32, e.shape, 0) + r
        e = jnp.where(i == lax.broadcasted_iota(jnp.int32, e.shape, 1), 0.0, e)
        e_all[0, rows, :] = e
        total[rows, :] = jnp.sum(e, axis=1, keepdims=True)
        score, p1 = score_tile(at[1], emb, peer, goal, rows)
        e = jnp.exp(score)
        e_all[1, rows, :] = e
        total[rows, :] += jnp.sum(e, axis=1, keepdims=True)
        pos[rows, :] = p0 + p1


def add_block(slot, emb, block, goal, e_all, total, pos):
    at = places()[slot]
    for r in range(0, emb.shape[0], WIDE):
        rows = pl.ds(r, WIDE)
        score, p = score_tile(at, emb, block, goal, rows)
        e = jnp.exp(score)
        e_all[slot, rows, :] = e
        total[rows, :] += jnp.sum(e, axis=1, keepdims=True)
        pos[rows, :] += p


def far(
    emb, even, odd, peer, goal, goal_row, token, e_in, total_in, pos_in, unit, rnorm,
    e_all, total, pos, unit_out, rnorm_out, note, part,
):
    def for_peer(block):
        for r in range(0, peer.shape[0], WIDE):
            rows = pl.ds(r, WIDE)
            e = jnp.exp(SCALE * dot_nt(peer[rows, :], block[...]))
            part[rows, :] = jnp.sum(e, axis=1, keepdims=True)

    pl.when(crossed())(lambda: for_peer(odd))
    pl.when(jnp.logical_not(crossed()))(lambda: for_peer(even))
    add_block(2, emb, even, goal, e_all, total, pos)
    add_block(3, emb, odd, goal, e_all, total, pos)
    note[0:1, :] = to_row(total[...])
    note[1:2, :] = to_row(part[...])
    note[2:3, :] = goal_row[...]
    note[3:4, :] = jnp.zeros_like(goal_row)


def combine(own, peer, pair, inverse):
    inv = 1.0 / (own[0:1, :] + peer[1:2, :])
    inverse[...] = to_column(inv)
    pair[0:1, :] = inv
    pair[1:2, :] = own[2:3, :]
    pair[2:3, :] = 1.0 / (peer[0:1, :] + own[1:2, :])
    pair[3:4, :] = peer[2:3, :]


def seal(emb, relay, goal, e_in, total_in, pos_in, unit, rnorm, e_all, total, pos, *kept):
    add_block(4, emb, relay, goal, e_all, total, pos)


def lose(total, pos, losses, token):
    losses[...] = to_row(jnp.log(total[...]) - pos[...])
    token[...] = jnp.zeros_like(token)


def slope(e, inverse, their_inverse, left, right):
    weight = e * (inverse + their_inverse)
    return jnp.where(left == right, weight - 1.0, weight)


def finish(
    base, goal, inverse, pair, even_note, odd_note, e_all, emb, peer, even, odd, relay, unit, rnorm, token,
    dz, g, acc,
):
    at = places()
    pair, even_note, odd_note = pair[...], even_note[...], odd_note[...]
    relay_note = jnp.where(crossed(), even_note, odd_note)[2:]
    notes = (pair[:2], pair[2:], even_note[:2], odd_note[:2], relay_note)
    blocks = (emb, peer, even, odd, relay)
    half, size = g.shape[1:]
    ids = lax.broadcasted_iota(jnp.int32, (1, size), 1)

    def slopes(k, rows):
        note = notes[k]
        their_inverse, their_goal = note[0:1], note[1:2].astype(jnp.int32)
        shift = at[k] * size
        ahead = at[k] >= 0
        right = jnp.where(ahead, ids + shift, their_goal + shift)
        mine = lax.broadcasted_iota(jnp.int32, (rows.size, 1), 0) + rows.start
        left = jnp.where(ahead, goal[rows, :], mine)
        weight = slope(e_all[k, rows, :], inverse[rows, :], their_inverse, left, right)
        if k == 0:
            weight = jnp.where(mine == their_goal, weight - 1.0, weight)
        g[k % 2, here(rows), :] = weight.astype(BF16)

    def here(rows):
        return pl.ds(rows.start - base, rows.size)

    tiles = [pl.ds(base + r, TILE) for r in range(0, half, TILE)]
    for rows in tiles:
        slopes(0, rows)
    for k, block in enumerate(blocks):
        product = dot(g[k % 2], block[...])
        if k + 1 < len(blocks):
            for rows in tiles:
                slopes(k + 1, rows)
        if k == 0:
            acc[...] = product
        else:
            acc[...] += product
    for rows in tiles:
        demb = SCALE * acc[here(rows), :]
        u = unit[rows, :]
        along = jnp.sum(u * demb, axis=1, keepdims=True)
        dz[here(rows), :] = ((demb - u * along) * rnorm[rows, :]).astype(BF16)


def turn(frames, token, mine, theirs):
    half, core = mine.shape[0], lax.axis_index("core")
    for out, k in ((mine, core), (theirs, 1 - core)):
        for c in range(0, half, 256):
            columns = pl.ds(pl.multiple_of(k * half + c, 128), 256)
            out[pl.ds(c, 256), :] = frames[:, columns].T


def add_up(got, out):
    total = got[0].astype(F32)
    for k in range(1, got.shape[0]):
        total += got[k].astype(F32)
    total = total.astype(BF16)
    for k in range(out.shape[0]):
        out[k] = total


def head_first(mine, theirs, dz_a, dz_b, other_a, out):
    n = dz_a.shape[0]
    out[...] = dot(mine[:, :n], dz_a[...]) + dot(theirs[:, :n], other_a[...]) + dot(mine[:, n:], dz_b[...])


def head_last(part, theirs, other_b, out):
    cut, n = out.shape[2], other_b.shape[0]
    for r in range(0, out.shape[1], WIDE):
        rows = pl.ds(r, WIDE)
        whole = part[rows, :] + dot(theirs[rows, n:], other_b[...])
        for k in range(2):
            out[k, rows, :] = whole[:, k * cut : (k + 1) * cut].astype(BF16)


def half_copies(part, out, sems, core):
    _, size, cut = part.shape
    step = size // 2
    start = pl.multiple_of(core * size, size)
    return [
        pltpu.make_async_copy(
            part.at[k, pl.ds(r * step, step), :],
            out.at[pl.ds(start + r * step, step), pl.ds(k * cut, cut)],
            sems.at[k, r],
        )
        for k in range(2)
        for r in range(2)
    ]


def ends(dz_a, dz_b, head, own, frame_grad, out, held, sems, out_sems):
    copies = half_copies(own, out, sems, lax.axis_index("core"))
    for c in copies:
        c.start()
    step = head.shape[0] // out_sems.shape[0]
    for k in range(out_sems.shape[0]):
        cut = pl.ds(k * step, step)
        n = dz_a.shape[0]
        held[:n, cut] = dot_nt(dz_a[...], head[cut, :]).astype(BF16)
        held[n:, cut] = dot_nt(dz_b[...], head[cut, :]).astype(BF16)
        copies.append(pltpu.make_async_copy(held.at[:, cut], frame_grad.at[:, cut], out_sems.at[k]))
        copies[-1].start()
    for c in copies:
        c.wait()


def last_half(other, whole, out, sems):
    copies = half_copies(other, out, sems, 1 - lax.axis_index("core"))
    for c in copies:
        c.start()
    for c in copies:
        c.wait()


def on_device(frames, head, offsets):
    rows, depth = frames.shape
    width = head.shape[1]
    shape = jax.ShapeDtypeStruct
    col, row = shape((rows, 1), F32), shape((1, rows), F32)
    square, tall = shape((rows, rows), F32), shape((rows, width), F32)
    note = shape((2, rows), F32)
    block_flops = 2 * rows * rows * width
    half = depth // 2
    vmem, hbm = pl.BlockSpec(memory_space=pltpu.VMEM), pl.BlockSpec(memory_space=pltpu.HBM)
    emb, unit, rnorm = pl.pallas_call(
        embed,
        in_specs=[hbm, hbm],
        out_specs=[vmem] * 3,
        out_shape=[shape((rows, width), BF16), tall, col],
        scratch_shapes=[
            pltpu.VMEM((rows, depth), BF16),
            pltpu.VMEM((depth, width), BF16),
            pltpu.VMEM((rows, width), F32),
            pltpu.SemaphoreType.DMA((2, 2)),
        ],
        name="embed",
        compiler_params=pltpu.CompilerParams(vmem_limit_bytes=51 * 2**20),
        cost_estimate=pl.CostEstimate(flops=2 * rows * depth * width, bytes_accessed=2**22, transcendentals=0),
    )(frames, head)

    peer = in_chip(emb)
    odd = swap_odd(emb)
    even = swap_even(emb)
    everything = shape((5, rows, rows), F32)
    e_all, total, pos, unit, rnorm, goal, goal_row = call(
        near, [everything, col, col, tall, col, shape((rows, 1), jnp.int32), row],
        emb, peer, offsets.reshape(1, rows), unit, rnorm,
        kept=((3, 3), (4, 4)), flops=2 * block_flops, name="near",
    )
    mine, theirs = call(turn, [shape((half, rows), BF16)] * 2, frames, pos, name="turn")
    theirs = in_chip(theirs)
    state, keep = [everything, col, col, tall, col], lambda k: tuple((k + j, j) for j in range(5))
    note = shape((4, rows), F32)
    e_all, total, pos, unit, rnorm, own_note = call(
        far, state + [note], emb, even, odd, peer, goal, goal_row, theirs, e_all, total, pos, unit, rnorm,
        kept=keep(7), scratch=[pltpu.VMEM((rows, 1), F32)], flops=3 * block_flops, name="far",
    )
    peer_note = in_chip(own_note)
    pair, inverse = call(combine, [note, col], own_note, peer_note, name="combine")
    odd_note = swap_odd(pair)
    even_note = swap_even(pair)
    (shared,) = call(pick, [shape((rows, width), BF16)], even, odd, pair, name="pick")
    relay = in_chip(shared)
    e_all, total, pos, unit, rnorm = call(
        seal, state, emb, relay, goal, e_all, total, pos, unit, rnorm, kept=keep(3), flops=block_flops, name="seal",
    )
    losses, token = call(lose, [row, shape((8, 128), F32)], total, pos, name="lose")
    parts = []
    for base in (0, rows // 2):
        (dz,) = call(
            functools.partial(finish, base), [shape((rows // 2, width), BF16)], goal, inverse, pair, even_note, odd_note,
            e_all, emb, peer, even, odd, relay, unit, rnorm, token,
            scratch=[pltpu.VMEM((2, rows // 2, rows), BF16), pltpu.VMEM((rows // 2, width), F32)],
            flops=5 * block_flops // 2, name="finish",
        )
        parts.append(dz)
        token = dz
    others = [in_chip(dz) for dz in parts]

    flops = 2 * half * rows * width
    (partial,) = call(
        head_first, [shape((half, width), F32)], mine, theirs, *parts, others[0], flops=flops, name="head_first"
    )
    (partial,) = call(
        head_last, [shape((2, half, width // 2), BF16)], partial, theirs, others[1], flops=flops, name="head_last"
    )
    share = (half // 16, width // 2)
    got = lax.all_to_all(partial.reshape(32, *share), NEAR, split_axis=0, concat_axis=0)
    (copies,) = call(add_up, [shape((4, *share), BF16)], got, name="add_near")
    got = lax.all_to_all(copies, "zh", split_axis=0, concat_axis=0)
    (copies,) = call(add_up, [shape((32, *share), BF16)], got, name="add_far")
    own = lax.all_to_all(copies, NEAR, split_axis=0, concat_axis=0).reshape(2, half, width // 2)
    other = in_chip(own)
    anywhere = pl.BlockSpec(memory_space=pl.ANY)
    frame_grad, head_grad = pl.pallas_call(
        ends,
        in_specs=[vmem, vmem, vmem, anywhere],
        out_specs=[anywhere] * 2,
        out_shape=[shape((rows, depth), BF16), shape((depth, width), BF16)],
        scratch_shapes=[
            pltpu.VMEM((rows, depth), BF16), pltpu.SemaphoreType.DMA((2, 2)), pltpu.SemaphoreType.DMA((3,))
        ],
        name="ends",
        compiler_params=pltpu.CompilerParams(vmem_limit_bytes=16 * 2**20),
        cost_estimate=pl.CostEstimate(flops=2 * rows * depth * width, bytes_accessed=2**22, transcendentals=0),
    )(*parts, head, own)
    head_grad = pl.pallas_call(
        last_half,
        in_specs=[anywhere] * 2,
        out_specs=anywhere,
        out_shape=shape((depth, width), BF16),
        scratch_shapes=[pltpu.SemaphoreType.DMA((2, 2))],
        input_output_aliases={1: 0},
        name="last_half",
        compiler_params=pltpu.CompilerParams(vmem_limit_bytes=2**20),
    )(other, head_grad)
    return (losses.reshape(rows), frame_grad, head_grad)


def solution(mesh):
    torus = Mesh(mesh.devices.reshape(SIZES), ALL)
    return jax.shard_map(
        on_device,
        mesh=torus,
        in_specs=(P(ALL, None), P(), P(ALL)),
        out_specs=(P(ALL), P(ALL, None), P()),
        check_vma=False,
    )
```

```python
import functools

import jax
import jax.numpy as jnp
from jax import lax
from jax.experimental import pallas as pl
from jax.experimental.pallas import tpu as pltpu
from jax.sharding import Mesh, PartitionSpec as P

SCALE = 50.0
ALL = ("zh", "zl", "y", "x", "core")
SIZES = (4, 2, 4, 4, 2)
NEAR = ("x", "y", "zl")
F32, BF16 = jnp.float32, jnp.bfloat16
TILE, WIDE = 128, 256


def send(x, to):
    return lax.ppermute(x, ALL, [(i, to(i) % 256) for i in range(256)])


def in_chip(x):
    return send(x, lambda i: i ^ 1)


def swap_even(x):
    return send(x, lambda i: i ^ 2)


def swap_odd(x):
    return send(x, lambda i: ((i + 2) ^ 2) - 2)


def dot(left, right):
    return jnp.dot(left, right, preferred_element_type=F32)


def dot_nt(left, right):
    return lax.dot_general(left, right, (((1,), (1,)), ((), ())), preferred_element_type=F32)


def to_row(column):
    return jnp.broadcast_to(column, (column.shape[0], 128)).T[:1]


def to_column(row):
    return jnp.broadcast_to(row, (128, row.shape[1])).T[:, :1]


def call(body, out, *arrays, scratch=(), flops=0, name=None, kept=()):
    vmem = pl.BlockSpec(memory_space=pltpu.VMEM)
    size = sum(a.size * a.dtype.itemsize for a in (*arrays, *out))
    return pl.pallas_call(
        body,
        out_shape=out,
        in_specs=[vmem] * len(arrays),
        out_specs=[vmem] * len(out),
        scratch_shapes=scratch,
        input_output_aliases=dict(kept),
        name=name,
        compiler_params=pltpu.CompilerParams(vmem_limit_bytes=16 * 2**20),
        cost_estimate=pl.CostEstimate(flops=flops, bytes_accessed=size, transcendentals=0),
    )(*arrays)


def embed(frames, head, emb, unit, rnorm, f, h, acc, sems):
    depth = head.shape[0]
    cuts = (pl.ds(0, depth // 2), pl.ds(depth // 2, depth // 2))
    copies = []
    for k, cut in enumerate(cuts):
        copies.append(pltpu.make_async_copy(frames.at[:, cut], f.at[:, cut], sems.at[0, k]))
        copies.append(pltpu.make_async_copy(head.at[cut, :], h.at[cut, :], sems.at[1, k]))
    for c in copies:
        c.start()
    copies[0].wait()
    copies[1].wait()
    acc[...] = dot(f[:, cuts[0]], h[cuts[0], :])
    copies[2].wait()
    copies[3].wait()
    cut = cuts[1]
    for r in range(0, acc.shape[0], WIDE):
        rows = pl.ds(r, WIDE)
        z = acc[rows, :] + dot(f[rows, cut], h[cut, :])
        norm = jnp.sqrt(jnp.sum(z * z, axis=1, keepdims=True) + 1e-06)
        inverse = 1.0 / norm
        u = z * inverse
        unit[rows, :] = u
        emb[rows, :] = u.astype(BF16)
        rnorm[rows, :] = inverse


def chip_sign():
    return 1 - 2 * lax.rem(lax.axis_index("x"), 2)


def crossed():
    return lax.rem(lax.axis_index("x") + lax.axis_index("core"), 2) == 1


def places():
    core = 1 - 2 * lax.axis_index("core")
    return (0, core, 2 * chip_sign(), -2 * chip_sign(), -core)


def pick(even, odd, token, out):
    out[...] = even[...]

    @pl.when(crossed())
    def _():
        out[...] = odd[...]


def score_tile(at, emb, block, goal, rows):
    score = SCALE * dot_nt(emb[rows, :], block[...])
    cols = lax.broadcasted_iota(jnp.int32, score.shape, 1) + at * block.shape[0]
    hit = cols == goal[rows, :]
    return score, jnp.sum(jnp.where(hit, score, 0.0), axis=1, keepdims=True)


def near(emb, peer, offsets, unit, rnorm, e_all, total, pos, unit_out, rnorm_out, goal, goal_row):
    at = places()
    positives = (offsets[...] + lax.broadcasted_iota(jnp.int32, offsets.shape, 1)).astype(F32)
    goal_row[...] = positives
    goal[...] = to_column(positives).astype(jnp.int32)
    for r in range(0, emb.shape[0], WIDE):
        rows = pl.ds(r, WIDE)
        score, p0 = score_tile(0, emb, emb, goal, rows)
        e = jnp.exp(score)
        i = lax.broadcasted_iota(jnp.int32, e.shape, 0) + r
        e = jnp.where(i == lax.broadcasted_iota(jnp.int32, e.shape, 1), 0.0, e)
        e_all[0, rows, :] = e
        total[rows, :] = jnp.sum(e, axis=1, keepdims=True)
        score, p1 = score_tile(at[1], emb, peer, goal, rows)
        e = jnp.exp(score)
        e_all[1, rows, :] = e
        total[rows, :] += jnp.sum(e, axis=1, keepdims=True)
        pos[rows, :] = p0 + p1


def add_block(slot, emb, block, goal, e_all, total, pos):
    at = places()[slot]
    for r in range(0, emb.shape[0], WIDE):
        rows = pl.ds(r, WIDE)
        score, p = score_tile(at, emb, block, goal, rows)
        e = jnp.exp(score)
        e_all[slot, rows, :] = e
        total[rows, :] += jnp.sum(e, axis=1, keepdims=True)
        pos[rows, :] += p


def far(
    emb, even, odd, peer, goal, goal_row, token, e_in, total_in, pos_in, unit, rnorm,
    e_all, total, pos, unit_out, rnorm_out, note, part,
):
    def for_peer(block):
        for r in range(0, peer.shape[0], WIDE):
            rows = pl.ds(r, WIDE)
            e = jnp.exp(SCALE * dot_nt(peer[rows, :], block[...]))
            part[rows, :] = jnp.sum(e, axis=1, keepdims=True)

    pl.when(crossed())(lambda: for_peer(odd))
    pl.when(jnp.logical_not(crossed()))(lambda: for_peer(even))
    add_block(2, emb, even, goal, e_all, total, pos)
    add_block(3, emb, odd, goal, e_all, total, pos)
    note[0:1, :] = to_row(total[...])
    note[1:2, :] = to_row(part[...])
    note[2:3, :] = goal_row[...]
    note[3:4, :] = jnp.zeros_like(goal_row)


def combine(own, peer, pair, inverse):
    inv = 1.0 / (own[0:1, :] + peer[1:2, :])
    inverse[...] = to_column(inv)
    pair[0:1, :] = inv
    pair[1:2, :] = own[2:3, :]
    pair[2:3, :] = 1.0 / (peer[0:1, :] + own[1:2, :])
    pair[3:4, :] = peer[2:3, :]


def seal(emb, relay, goal, e_in, total_in, pos_in, unit, rnorm, e_all, total, pos, *kept):
    add_block(4, emb, relay, goal, e_all, total, pos)


def lose(total, pos, losses, token):
    losses[...] = to_row(jnp.log(total[...]) - pos[...])
    token[...] = jnp.zeros_like(token)


def slope(e, inverse, their_inverse, left, right):
    weight = e * (inverse + their_inverse)
    return jnp.where(left == right, weight - 1.0, weight)


def finish(
    base, goal, inverse, pair, even_note, odd_note, e_all, emb, peer, even, odd, relay, unit, rnorm, token,
    dz, g, acc,
):
    at = places()
    pair, even_note, odd_note = pair[...], even_note[...], odd_note[...]
    relay_note = jnp.where(crossed(), even_note, odd_note)[2:]
    notes = (pair[:2], pair[2:], even_note[:2], odd_note[:2], relay_note)
    blocks = (emb, peer, even, odd, relay)
    half, size = g.shape[1:]
    ids = lax.broadcasted_iota(jnp.int32, (1, size), 1)

    def slopes(k, rows):
        note = notes[k]
        their_inverse, their_goal = note[0:1], note[1:2].astype(jnp.int32)
        shift = at[k] * size
        ahead = at[k] >= 0
        right = jnp.where(ahead, ids + shift, their_goal + shift)
        mine = lax.broadcasted_iota(jnp.int32, (rows.size, 1), 0) + rows.start
        left = jnp.where(ahead, goal[rows, :], mine)
        weight = slope(e_all[k, rows, :], inverse[rows, :], their_inverse, left, right)
        if k == 0:
            weight = jnp.where(mine == their_goal, weight - 1.0, weight)
        g[k % 2, here(rows), :] = weight.astype(BF16)

    def here(rows):
        return pl.ds(rows.start - base, rows.size)

    tiles = [pl.ds(base + r, TILE) for r in range(0, half, TILE)]
    for rows in tiles:
        slopes(0, rows)
    for k, block in enumerate(blocks):
        product = dot(g[k % 2], block[...])
        if k + 1 < len(blocks):
            for rows in tiles:
                slopes(k + 1, rows)
        if k == 0:
            acc[...] = product
        else:
            acc[...] += product
    for rows in tiles:
        demb = SCALE * acc[here(rows), :]
        u = unit[rows, :]
        along = jnp.sum(u * demb, axis=1, keepdims=True)
        dz[here(rows), :] = ((demb - u * along) * rnorm[rows, :]).astype(BF16)


def turn(frames, token, mine, theirs):
    half, core = mine.shape[0], lax.axis_index("core")
    for out, k in ((mine, core), (theirs, 1 - core)):
        for c in range(0, half, 256):
            columns = pl.ds(pl.multiple_of(k * half + c, 128), 256)
            out[pl.ds(c, 256), :] = frames[:, columns].T


def add_up(got, out):
    total = got[0].astype(F32)
    for k in range(1, got.shape[0]):
        total += got[k].astype(F32)
    total = total.astype(BF16)
    for k in range(out.shape[0]):
        out[k] = total


def head_first(mine, theirs, dz_a, dz_b, other_a, out):
    n = dz_a.shape[0]
    out[...] = dot(mine[:, :n], dz_a[...]) + dot(theirs[:, :n], other_a[...]) + dot(mine[:, n:], dz_b[...])


def head_last(part, theirs, other_b, out):
    cut, n = out.shape[2], other_b.shape[0]
    for r in range(0, out.shape[1], WIDE):
        rows = pl.ds(r, WIDE)
        whole = part[rows, :] + dot(theirs[rows, n:], other_b[...])
        for k in range(2):
            out[k, rows, :] = whole[:, k * cut : (k + 1) * cut].astype(BF16)


def half_copies(part, out, sems, core):
    _, size, cut = part.shape
    step = size // 2
    start = pl.multiple_of(core * size, size)
    return [
        pltpu.make_async_copy(
            part.at[k, pl.ds(r * step, step), :],
            out.at[pl.ds(start + r * step, step), pl.ds(k * cut, cut)],
            sems.at[k, r],
        )
        for k in range(2)
        for r in range(2)
    ]


def ends(dz_a, dz_b, head, own, frame_grad, out, held, sems, out_sems):
    copies = half_copies(own, out, sems, lax.axis_index("core"))
    for c in copies:
        c.start()
    step = head.shape[0] // out_sems.shape[0]
    for k in range(out_sems.shape[0]):
        cut = pl.ds(k * step, step)
        n = dz_a.shape[0]
        held[:n, cut] = dot_nt(dz_a[...], head[cut, :]).astype(BF16)
        held[n:, cut] = dot_nt(dz_b[...], head[cut, :]).astype(BF16)
        copies.append(pltpu.make_async_copy(held.at[:, cut], frame_grad.at[:, cut], out_sems.at[k]))
        copies[-1].start()
    for c in copies:
        c.wait()


def last_half(other, whole, out, sems):
    copies = half_copies(other, out, sems, 1 - lax.axis_index("core"))
    for c in copies:
        c.start()
    for c in copies:
        c.wait()


def on_device(frames, head, offsets):
    rows, depth = frames.shape
    width = head.shape[1]
    shape = jax.ShapeDtypeStruct
    col, row = shape((rows, 1), F32), shape((1, rows), F32)
    square, tall = shape((rows, rows), F32), shape((rows, width), F32)
    note = shape((2, rows), F32)
    block_flops = 2 * rows * rows * width
    half = depth // 2
    vmem, hbm = pl.BlockSpec(memory_space=pltpu.VMEM), pl.BlockSpec(memory_space=pltpu.HBM)
    emb, unit, rnorm = pl.pallas_call(
        embed,
        in_specs=[hbm, hbm],
        out_specs=[vmem] * 3,
        out_shape=[shape((rows, width), BF16), tall, col],
        scratch_shapes=[
            pltpu.VMEM((rows, depth), BF16),
            pltpu.VMEM((depth, width), BF16),
            pltpu.VMEM((rows, width), F32),
            pltpu.SemaphoreType.DMA((2, 2)),
        ],
        name="embed",
        compiler_params=pltpu.CompilerParams(vmem_limit_bytes=51 * 2**20),
        cost_estimate=pl.CostEstimate(flops=2 * rows * depth * width, bytes_accessed=2**22, transcendentals=0),
    )(frames, head)

    peer = in_chip(emb)
    odd = swap_odd(emb)
    even = swap_even(emb)
    everything = shape((5, rows, rows), F32)
    e_all, total, pos, unit, rnorm, goal, goal_row = call(
        near, [everything, col, col, tall, col, shape((rows, 1), jnp.int32), row],
        emb, peer, offsets.reshape(1, rows), unit, rnorm,
        kept=((3, 3), (4, 4)), flops=2 * block_flops, name="near",
    )
    mine, theirs = call(turn, [shape((half, rows), BF16)] * 2, frames, pos, name="turn")
    theirs = in_chip(theirs)
    state, keep = [everything, col, col, tall, col], lambda k: tuple((k + j, j) for j in range(5))
    note = shape((4, rows), F32)
    e_all, total, pos, unit, rnorm, own_note = call(
        far, state + [note], emb, even, odd, peer, goal, goal_row, theirs, e_all, total, pos, unit, rnorm,
        kept=keep(7), scratch=[pltpu.VMEM((rows, 1), F32)], flops=3 * block_flops, name="far",
    )
    peer_note = in_chip(own_note)
    pair, inverse = call(combine, [note, col], own_note, peer_note, name="combine")
    odd_note = swap_odd(pair)
    even_note = swap_even(pair)
    (shared,) = call(pick, [shape((rows, width), BF16)], even, odd, pair, name="pick")
    relay = in_chip(shared)
    e_all, total, pos, unit, rnorm = call(
        seal, state, emb, relay, goal, e_all, total, pos, unit, rnorm, kept=keep(3), flops=block_flops, name="seal",
    )
    losses, token = call(lose, [row, shape((8, 128), F32)], total, pos, name="lose")
    parts = []
    for base in (0, rows // 2):
        (dz,) = call(
            functools.partial(finish, base), [shape((rows // 2, width), BF16)], goal, inverse, pair, even_note, odd_note,
            e_all, emb, peer, even, odd, relay, unit, rnorm, token,
            scratch=[pltpu.VMEM((2, rows // 2, rows), BF16), pltpu.VMEM((rows // 2, width), F32)],
            flops=5 * block_flops // 2, name="finish",
        )
        parts.append(dz)
        token = dz
    others = [in_chip(dz) for dz in parts]

    flops = 2 * half * rows * width
    (partial,) = call(
        head_first, [shape((half, width), F32)], mine, theirs, *parts, others[0], flops=flops, name="head_first"
    )
    (partial,) = call(
        head_last, [shape((2, half, width // 2), BF16)], partial, theirs, others[1], flops=flops, name="head_last"
    )
    share = (half // 16, width // 2)
    got = lax.all_to_all(partial.reshape(32, *share), NEAR, split_axis=0, concat_axis=0)
    (copies,) = call(add_up, [shape((4, *share), BF16)], got, name="add_near")
    got = lax.all_to_all(copies, "zh", split_axis=0, concat_axis=0)
    (copies,) = call(add_up, [shape((32, *share), BF16)], got, name="add_far")
    own = lax.all_to_all(copies, NEAR, split_axis=0, concat_axis=0).reshape(2, half, width // 2)
    other = in_chip(own)
    anywhere = pl.BlockSpec(memory_space=pl.ANY)
    frame_grad, head_grad = pl.pallas_call(
        ends,
        in_specs=[vmem, vmem, vmem, anywhere],
        out_specs=[anywhere] * 2,
        out_shape=[shape((rows, depth), BF16), shape((depth, width), BF16)],
        scratch_shapes=[
            pltpu.VMEM((rows, depth), BF16), pltpu.SemaphoreType.DMA((2, 2)), pltpu.SemaphoreType.DMA((3,))
        ],
        name="ends",
        compiler_params=pltpu.CompilerParams(vmem_limit_bytes=16 * 2**20),
        cost_estimate=pl.CostEstimate(flops=2 * rows * depth * width, bytes_accessed=2**22, transcendentals=0),
    )(*parts, head, own)
    head_grad = pl.pallas_call(
        last_half,
        in_specs=[anywhere] * 2,
        out_specs=anywhere,
        out_shape=shape((depth, width), BF16),
        scratch_shapes=[pltpu.SemaphoreType.DMA((2, 2))],
        input_output_aliases={1: 0},
        name="last_half",
        compiler_params=pltpu.CompilerParams(vmem_limit_bytes=2**20),
    )(other, head_grad)
    return (losses.reshape(rows), frame_grad, head_grad)


def solution(mesh):
    torus = Mesh(mesh.devices.reshape(SIZES), ALL)
    return jax.shard_map(
        on_device,
        mesh=torus,
        in_specs=(P(ALL, None), P(), P(ALL)),
        out_specs=(P(ALL), P(ALL, None), P()),
        check_vma=False,
    )
```

```python
import functools

import jax
import jax.numpy as jnp
from jax import lax
from jax.experimental import pallas as pl
from jax.experimental.pallas import tpu as pltpu
from jax.sharding import Mesh, PartitionSpec as P

SCALE = 50.0
ALL = ("zh", "zl", "y", "x", "core")
SIZES = (4, 2, 4, 4, 2)
NEAR = ("zl", "y", "x")
F32, BF16 = jnp.float32, jnp.bfloat16
TILE, WIDE, SCORES = 128, 256, 512


def send(x, to):
    return lax.ppermute(x, ALL, [(i, to(i) % 256) for i in range(256)])


def in_chip(x):
    return send(x, lambda i: i ^ 1)


def swap_even(x):
    return send(x, lambda i: i ^ 2)


def swap_odd(x):
    return send(x, lambda i: ((i + 2) ^ 2) - 2)


def dot(left, right):
    return jnp.dot(left, right, preferred_element_type=F32)


def dot_nt(left, right):
    return lax.dot_general(left, right, (((1,), (1,)), ((), ())), preferred_element_type=F32)


def to_row(column):
    return jnp.broadcast_to(column, (column.shape[0], 128)).T[:1]


def to_column(row):
    return jnp.broadcast_to(row, (128, row.shape[1])).T[:, :1]


def call(body, out, *arrays, scratch=(), flops=0, name=None, kept=()):
    vmem = pl.BlockSpec(memory_space=pltpu.VMEM)
    size = sum(a.size * a.dtype.itemsize for a in (*arrays, *out))
    return pl.pallas_call(
        body,
        out_shape=out,
        in_specs=[vmem] * len(arrays),
        out_specs=[vmem] * len(out),
        scratch_shapes=scratch,
        input_output_aliases=dict(kept),
        name=name,
        compiler_params=pltpu.CompilerParams(vmem_limit_bytes=16 * 2**20),
        cost_estimate=pl.CostEstimate(flops=flops, bytes_accessed=size, transcendentals=0),
    )(*arrays)


def embed(frames, head, emb, unit, rnorm, f, h, acc, sems):
    depth = head.shape[0]
    cuts = (pl.ds(0, depth // 2), pl.ds(depth // 2, depth // 2))
    copies = []
    for k, cut in enumerate(cuts):
        copies.append(pltpu.make_async_copy(frames.at[:, cut], f.at[:, cut], sems.at[0, k]))
        copies.append(pltpu.make_async_copy(head.at[cut, :], h.at[cut, :], sems.at[1, k]))
    for c in copies:
        c.start()
    copies[0].wait()
    copies[1].wait()
    acc[...] = dot(f[:, cuts[0]], h[cuts[0], :])
    copies[2].wait()
    copies[3].wait()
    cut = cuts[1]
    for r in range(0, acc.shape[0], WIDE):
        rows = pl.ds(r, WIDE)
        z = acc[rows, :] + dot(f[rows, cut], h[cut, :])
        norm = jnp.sqrt(jnp.sum(z * z, axis=1, keepdims=True) + 1e-06)
        inverse = 1.0 / norm
        u = z * inverse
        unit[rows, :] = u
        emb[rows, :] = u.astype(BF16)
        rnorm[rows, :] = inverse


def chip_sign():
    return 1 - 2 * lax.rem(lax.axis_index("x"), 2)


def crossed():
    return lax.rem(lax.axis_index("x") + lax.axis_index("core"), 2) == 1


def places():
    core = 1 - 2 * lax.axis_index("core")
    return (0, core, 2 * chip_sign(), -2 * chip_sign(), -core)


def pick(even, odd, token, out):
    out[...] = even[...]

    @pl.when(crossed())
    def _():
        out[...] = odd[...]


def score_tile(at, emb, block, goal, rows):
    score = SCALE * dot_nt(emb[rows, :], block[...])
    cols = lax.broadcasted_iota(jnp.int32, score.shape, 1) + at * block.shape[0]
    hit = cols == goal[rows, :]
    return score, jnp.sum(jnp.where(hit, score, 0.0), axis=1, keepdims=True)


def near(emb, peer, offsets, unit, rnorm, e_all, total, pos, unit_out, rnorm_out, goal, goal_row):
    at = places()
    positives = (offsets[...] + lax.broadcasted_iota(jnp.int32, offsets.shape, 1)).astype(F32)
    goal_row[...] = positives
    goal[...] = to_column(positives).astype(jnp.int32)
    for r in range(0, emb.shape[0], SCORES):
        rows = pl.ds(r, SCORES)
        score, p0 = score_tile(0, emb, emb, goal, rows)
        e = jnp.exp(score)
        i = lax.broadcasted_iota(jnp.int32, e.shape, 0) + r
        e = jnp.where(i == lax.broadcasted_iota(jnp.int32, e.shape, 1), 0.0, e)
        e_all[0, rows, :] = e
        total[rows, :] = jnp.sum(e, axis=1, keepdims=True)
        score, p1 = score_tile(at[1], emb, peer, goal, rows)
        e = jnp.exp(score)
        e_all[1, rows, :] = e
        total[rows, :] += jnp.sum(e, axis=1, keepdims=True)
        pos[rows, :] = p0 + p1


def add_block(slot, emb, block, goal, e_all, total, pos):
    at = places()[slot]
    for r in range(0, emb.shape[0], SCORES):
        rows = pl.ds(r, SCORES)
        score, p = score_tile(at, emb, block, goal, rows)
        e = jnp.exp(score)
        e_all[slot, rows, :] = e
        total[rows, :] += jnp.sum(e, axis=1, keepdims=True)
        pos[rows, :] += p


def far(
    emb, even, odd, peer, goal, goal_row, token, e_in, total_in, pos_in, unit, rnorm,
    e_all, total, pos, unit_out, rnorm_out, note, part,
):
    def for_peer(block):
        for r in range(0, peer.shape[0], SCORES):
            rows = pl.ds(r, SCORES)
            e = jnp.exp(SCALE * dot_nt(peer[rows, :], block[...]))
            part[rows, :] = jnp.sum(e, axis=1, keepdims=True)

    pl.when(crossed())(lambda: for_peer(odd))
    pl.when(jnp.logical_not(crossed()))(lambda: for_peer(even))
    add_block(2, emb, even, goal, e_all, total, pos)
    add_block(3, emb, odd, goal, e_all, total, pos)
    note[0:1, :] = to_row(total[...])
    note[1:2, :] = to_row(part[...])
    note[2:3, :] = goal_row[...]
    note[3:4, :] = jnp.zeros_like(goal_row)


def combine(own, peer, pair, inverse):
    inv = 1.0 / (own[0:1, :] + peer[1:2, :])
    inverse[...] = to_column(inv)
    pair[0:1, :] = inv
    pair[1:2, :] = own[2:3, :]
    pair[2:3, :] = 1.0 / (peer[0:1, :] + own[1:2, :])
    pair[3:4, :] = peer[2:3, :]


def seal(emb, relay, goal, e_in, total_in, pos_in, unit, rnorm, e_all, total, pos, *kept):
    add_block(4, emb, relay, goal, e_all, total, pos)


def lose(total, pos, losses, token):
    losses[...] = to_row(jnp.log(total[...]) - pos[...])
    token[...] = jnp.zeros_like(token)


def slope(e, inverse, their_inverse, left, right):
    weight = e * (inverse + their_inverse)
    return jnp.where(left == right, weight - 1.0, weight)


def finish(
    base, goal, inverse, pair, even_note, odd_note, e_all, emb, peer, even, odd, relay, unit, rnorm, token,
    dz, g, acc,
):
    at = places()
    pair, even_note, odd_note = pair[...], even_note[...], odd_note[...]
    relay_note = jnp.where(crossed(), even_note, odd_note)[2:]
    notes = (pair[:2], pair[2:], even_note[:2], odd_note[:2], relay_note)
    blocks = (emb, peer, even, odd, relay)
    half, size = g.shape[1:]
    ids = lax.broadcasted_iota(jnp.int32, (1, size), 1)

    def slopes(k, rows):
        note = notes[k]
        their_inverse, their_goal = note[0:1], note[1:2].astype(jnp.int32)
        shift = at[k] * size
        ahead = at[k] >= 0
        right = jnp.where(ahead, ids + shift, their_goal + shift)
        mine = lax.broadcasted_iota(jnp.int32, (rows.size, 1), 0) + rows.start
        left = jnp.where(ahead, goal[rows, :], mine)
        weight = slope(e_all[k, rows, :], inverse[rows, :], their_inverse, left, right)
        if k == 0:
            weight = jnp.where(mine == their_goal, weight - 1.0, weight)
        g[k % 2, here(rows), :] = weight.astype(BF16)

    def here(rows):
        return pl.ds(rows.start - base, rows.size)

    tiles = [pl.ds(base + r, TILE) for r in range(0, half, TILE)]
    for rows in tiles:
        slopes(0, rows)
    for k, block in enumerate(blocks):
        product = dot(g[k % 2], block[...])
        if k + 1 < len(blocks):
            for rows in tiles:
                slopes(k + 1, rows)
        if k == 0:
            acc[...] = product
        else:
            acc[...] += product
    for rows in tiles:
        demb = SCALE * acc[here(rows), :]
        u = unit[rows, :]
        along = jnp.sum(u * demb, axis=1, keepdims=True)
        dz[here(rows), :] = ((demb - u * along) * rnorm[rows, :]).astype(BF16)


def turn(frames, token, mine, theirs):
    half, core = mine.shape[0], lax.axis_index("core")
    for out, k in ((mine, core), (theirs, 1 - core)):
        for c in range(0, half, 256):
            columns = pl.ds(pl.multiple_of(k * half + c, 128), 256)
            out[pl.ds(c, 256), :] = frames[:, columns].T


def add_up(got, out):
    total = got[0].astype(F32)
    for k in range(1, got.shape[0]):
        total += got[k].astype(F32)
    total = total.astype(BF16)
    for k in range(out.shape[0]):
        out[k] = total


def head_first(mine, theirs, dz_a, dz_b, other_a, out):
    n = dz_a.shape[0]
    out[...] = dot(mine[:, :n], dz_a[...]) + dot(theirs[:, :n], other_a[...]) + dot(mine[:, n:], dz_b[...])


def head_last(part, theirs, other_b, out):
    cut, n = out.shape[2], other_b.shape[0]
    for r in range(0, out.shape[1], WIDE):
        rows = pl.ds(r, WIDE)
        whole = part[rows, :] + dot(theirs[rows, n:], other_b[...])
        for k in range(2):
            out[k, rows, :] = whole[:, k * cut : (k + 1) * cut].astype(BF16)


def half_copies(part, out, sems, core):
    _, size, cut = part.shape
    step = size // 2
    start = pl.multiple_of(core * size, size)
    return [
        pltpu.make_async_copy(
            part.at[k, pl.ds(r * step, step), :],
            out.at[pl.ds(start + r * step, step), pl.ds(k * cut, cut)],
            sems.at[k, r],
        )
        for k in range(2)
        for r in range(2)
    ]


def ends(dz_a, dz_b, head, own, frame_grad, out, held, sems, out_sems):
    copies = half_copies(own, out, sems, lax.axis_index("core"))
    for c in copies:
        c.start()
    step = head.shape[0] // out_sems.shape[0]
    for k in range(out_sems.shape[0]):
        cut = pl.ds(k * step, step)
        n = dz_a.shape[0]
        held[:n, cut] = dot_nt(dz_a[...], head[cut, :]).astype(BF16)
        held[n:, cut] = dot_nt(dz_b[...], head[cut, :]).astype(BF16)
        copies.append(pltpu.make_async_copy(held.at[:, cut], frame_grad.at[:, cut], out_sems.at[k]))
        copies[-1].start()
    for c in copies:
        c.wait()


def last_half(other, whole, out, sems):
    copies = half_copies(other, out, sems, 1 - lax.axis_index("core"))
    for c in copies:
        c.start()
    for c in copies:
        c.wait()


def on_device(frames, head, offsets):
    rows, depth = frames.shape
    width = head.shape[1]
    shape = jax.ShapeDtypeStruct
    col, row = shape((rows, 1), F32), shape((1, rows), F32)
    square, tall = shape((rows, rows), F32), shape((rows, width), F32)
    note = shape((2, rows), F32)
    block_flops = 2 * rows * rows * width
    half = depth // 2
    vmem, hbm = pl.BlockSpec(memory_space=pltpu.VMEM), pl.BlockSpec(memory_space=pltpu.HBM)
    emb, unit, rnorm = pl.pallas_call(
        embed,
        in_specs=[hbm, hbm],
        out_specs=[vmem] * 3,
        out_shape=[shape((rows, width), BF16), tall, col],
        scratch_shapes=[
            pltpu.VMEM((rows, depth), BF16),
            pltpu.VMEM((depth, width), BF16),
            pltpu.VMEM((rows, width), F32),
            pltpu.SemaphoreType.DMA((2, 2)),
        ],
        name="embed",
        compiler_params=pltpu.CompilerParams(vmem_limit_bytes=51 * 2**20),
        cost_estimate=pl.CostEstimate(flops=2 * rows * depth * width, bytes_accessed=2**22, transcendentals=0),
    )(frames, head)

    peer = in_chip(emb)
    odd = swap_odd(emb)
    even = swap_even(emb)
    everything = shape((5, rows, rows), F32)
    e_all, total, pos, unit, rnorm, goal, goal_row = call(
        near, [everything, col, col, tall, col, shape((rows, 1), jnp.int32), row],
        emb, peer, offsets.reshape(1, rows), unit, rnorm,
        kept=((3, 3), (4, 4)), flops=2 * block_flops, name="near",
    )
    mine, theirs = call(turn, [shape((half, rows), BF16)] * 2, frames, pos, name="turn")
    theirs = in_chip(theirs)
    state, keep = [everything, col, col, tall, col], lambda k: tuple((k + j, j) for j in range(5))
    note = shape((4, rows), F32)
    e_all, total, pos, unit, rnorm, own_note = call(
        far, state + [note], emb, even, odd, peer, goal, goal_row, theirs, e_all, total, pos, unit, rnorm,
        kept=keep(7), scratch=[pltpu.VMEM((rows, 1), F32)], flops=3 * block_flops, name="far",
    )
    peer_note = in_chip(own_note)
    pair, inverse = call(combine, [note, col], own_note, peer_note, name="combine")
    odd_note = swap_odd(pair)
    even_note = swap_even(pair)
    (shared,) = call(pick, [shape((rows, width), BF16)], even, odd, pair, name="pick")
    relay = in_chip(shared)
    e_all, total, pos, unit, rnorm = call(
        seal, state, emb, relay, goal, e_all, total, pos, unit, rnorm, kept=keep(3), flops=block_flops, name="seal",
    )
    losses, token = call(lose, [row, shape((8, 128), F32)], total, pos, name="lose")
    parts = []
    for base in (0, rows // 2):
        (dz,) = call(
            functools.partial(finish, base), [shape((rows // 2, width), BF16)], goal, inverse, pair, even_note, odd_note,
            e_all, emb, peer, even, odd, relay, unit, rnorm, token,
            scratch=[pltpu.VMEM((2, rows // 2, rows), BF16), pltpu.VMEM((rows // 2, width), F32)],
            flops=5 * block_flops // 2, name="finish",
        )
        parts.append(dz)
        token = dz
    others = [in_chip(dz) for dz in parts]

    flops = 2 * half * rows * width
    (partial,) = call(
        head_first, [shape((half, width), F32)], mine, theirs, *parts, others[0], flops=flops, name="head_first"
    )
    (partial,) = call(
        head_last, [shape((2, half, width // 2), BF16)], partial, theirs, others[1], flops=flops, name="head_last"
    )
    share = (half // 16, width // 2)
    got = lax.all_to_all(partial.reshape(32, *share), NEAR, split_axis=0, concat_axis=0)
    (copies,) = call(add_up, [shape((4, *share), BF16)], got, name="add_near")
    got = lax.all_to_all(copies, "zh", split_axis=0, concat_axis=0)
    (copies,) = call(add_up, [shape((32, *share), BF16)], got, name="add_far")
    own = lax.all_to_all(copies, NEAR, split_axis=0, concat_axis=0).reshape(2, half, width // 2)
    other = in_chip(own)
    anywhere = pl.BlockSpec(memory_space=pl.ANY)
    frame_grad, head_grad = pl.pallas_call(
        ends,
        in_specs=[vmem, vmem, vmem, anywhere],
        out_specs=[anywhere] * 2,
        out_shape=[shape((rows, depth), BF16), shape((depth, width), BF16)],
        scratch_shapes=[
            pltpu.VMEM((rows, depth), BF16), pltpu.SemaphoreType.DMA((2, 2)), pltpu.SemaphoreType.DMA((3,))
        ],
        name="ends",
        compiler_params=pltpu.CompilerParams(vmem_limit_bytes=16 * 2**20),
        cost_estimate=pl.CostEstimate(flops=2 * rows * depth * width, bytes_accessed=2**22, transcendentals=0),
    )(*parts, head, own)
    head_grad = pl.pallas_call(
        last_half,
        in_specs=[anywhere] * 2,
        out_specs=anywhere,
        out_shape=shape((depth, width), BF16),
        scratch_shapes=[pltpu.SemaphoreType.DMA((2, 2))],
        input_output_aliases={1: 0},
        name="last_half",
        compiler_params=pltpu.CompilerParams(vmem_limit_bytes=2**20),
    )(other, head_grad)
    return (losses.reshape(rows), frame_grad, head_grad)


def solution(mesh):
    torus = Mesh(mesh.devices.reshape(SIZES), ALL)
    return jax.shard_map(
        on_device,
        mesh=torus,
        in_specs=(P(ALL, None), P(), P(ALL)),
        out_specs=(P(ALL), P(ALL, None), P()),
        check_vma=False,
    )
```

```python
import functools

import jax
import jax.numpy as jnp
from jax import lax
from jax.experimental import pallas as pl
from jax.experimental.pallas import tpu as pltpu
from jax.sharding import Mesh, PartitionSpec as P

SCALE = 50.0
ALL = ("zh", "zl", "y", "x", "core")
SIZES = (4, 2, 4, 4, 2)
NEAR = ("zl", "y", "x")
F32, BF16 = jnp.float32, jnp.bfloat16
TILE, WIDE = 128, 256


def send(x, to):
    return lax.ppermute(x, ALL, [(i, to(i) % 256) for i in range(256)])


def in_chip(x):
    return send(x, lambda i: i ^ 1)


def swap_even(x):
    return send(x, lambda i: i ^ 2)


def swap_odd(x):
    return send(x, lambda i: ((i + 2) ^ 2) - 2)


def dot(left, right):
    return jnp.dot(left, right, preferred_element_type=F32)


def dot_nt(left, right):
    return lax.dot_general(left, right, (((1,), (1,)), ((), ())), preferred_element_type=F32)


def to_row(column):
    return jnp.broadcast_to(column, (column.shape[0], 128)).T[:1]


def to_column(row):
    return jnp.broadcast_to(row, (128, row.shape[1])).T[:, :1]


def call(body, out, *arrays, scratch=(), flops=0, name=None, kept=()):
    vmem = pl.BlockSpec(memory_space=pltpu.VMEM)
    size = sum(a.size * a.dtype.itemsize for a in (*arrays, *out))
    return pl.pallas_call(
        body,
        out_shape=out,
        in_specs=[vmem] * len(arrays),
        out_specs=[vmem] * len(out),
        scratch_shapes=scratch,
        input_output_aliases=dict(kept),
        name=name,
        compiler_params=pltpu.CompilerParams(vmem_limit_bytes=16 * 2**20),
        cost_estimate=pl.CostEstimate(flops=flops, bytes_accessed=size, transcendentals=0),
    )(*arrays)


def embed(frames, head, emb, unit, rnorm, f, h, acc, sems):
    depth = head.shape[0]
    cuts = (pl.ds(0, depth // 2), pl.ds(depth // 2, depth // 2))
    copies = []
    for k, cut in enumerate(cuts):
        copies.append(pltpu.make_async_copy(frames.at[:, cut], f.at[:, cut], sems.at[0, k]))
        copies.append(pltpu.make_async_copy(head.at[cut, :], h.at[cut, :], sems.at[1, k]))
    for c in copies:
        c.start()
    copies[0].wait()
    copies[1].wait()
    acc[...] = dot(f[:, cuts[0]], h[cuts[0], :])
    copies[2].wait()
    copies[3].wait()
    cut = cuts[1]
    for r in range(0, acc.shape[0], WIDE):
        rows = pl.ds(r, WIDE)
        z = acc[rows, :] + dot(f[rows, cut], h[cut, :])
        norm = jnp.sqrt(jnp.sum(z * z, axis=1, keepdims=True) + 1e-06)
        inverse = 1.0 / norm
        u = z * inverse
        unit[rows, :] = u
        emb[rows, :] = u.astype(BF16)
        rnorm[rows, :] = inverse


def chip_sign():
    return 1 - 2 * lax.rem(lax.axis_index("x"), 2)


def crossed():
    return lax.rem(lax.axis_index("x") + lax.axis_index("core"), 2) == 1


def places():
    core = 1 - 2 * lax.axis_index("core")
    return (0, core, 2 * chip_sign(), -2 * chip_sign(), -core)


def pick(even, odd, token, out):
    out[...] = even[...]

    @pl.when(crossed())
    def _():
        out[...] = odd[...]


def score_tile(at, emb, block, goal, rows):
    score = SCALE * dot_nt(emb[rows, :], block[...])
    cols = lax.broadcasted_iota(jnp.int32, score.shape, 1) + at * block.shape[0]
    hit = cols == goal[rows, :]
    return score, jnp.sum(jnp.where(hit, score, 0.0), axis=1, keepdims=True)


def near(emb, peer, offsets, unit, rnorm, e_all, total, pos, unit_out, rnorm_out, goal, goal_row):
    at = places()
    positives = (offsets[...] + lax.broadcasted_iota(jnp.int32, offsets.shape, 1)).astype(F32)
    goal_row[...] = positives
    goal[...] = to_column(positives).astype(jnp.int32)
    for r in range(0, emb.shape[0], WIDE):
        rows = pl.ds(r, WIDE)
        score, p0 = score_tile(0, emb, emb, goal, rows)
        e = jnp.exp(score)
        i = lax.broadcasted_iota(jnp.int32, e.shape, 0) + r
        e = jnp.where(i == lax.broadcasted_iota(jnp.int32, e.shape, 1), 0.0, e)
        e_all[0, rows, :] = e
        total[rows, :] = jnp.sum(e, axis=1, keepdims=True)
        score, p1 = score_tile(at[1], emb, peer, goal, rows)
        e = jnp.exp(score)
        e_all[1, rows, :] = e
        total[rows, :] += jnp.sum(e, axis=1, keepdims=True)
        pos[rows, :] = p0 + p1


def add_block(slot, emb, block, goal, e_all, total, pos):
    at = places()[slot]
    for r in range(0, emb.shape[0], WIDE):
        rows = pl.ds(r, WIDE)
        score, p = score_tile(at, emb, block, goal, rows)
        e = jnp.exp(score)
        e_all[slot, rows, :] = e
        total[rows, :] += jnp.sum(e, axis=1, keepdims=True)
        pos[rows, :] += p


def far(
    emb, even, odd, peer, goal, goal_row, token, e_in, total_in, pos_in, unit, rnorm,
    e_all, total, pos, unit_out, rnorm_out, note, part,
):
    def for_peer(block):
        for r in range(0, peer.shape[0], WIDE):
            rows = pl.ds(r, WIDE)
            e = jnp.exp(SCALE * dot_nt(peer[rows, :], block[...]))
            part[rows, :] = jnp.sum(e, axis=1, keepdims=True)

    pl.when(crossed())(lambda: for_peer(odd))
    pl.when(jnp.logical_not(crossed()))(lambda: for_peer(even))
    add_block(2, emb, even, goal, e_all, total, pos)
    add_block(3, emb, odd, goal, e_all, total, pos)
    note[0:1, :] = to_row(total[...])
    note[1:2, :] = to_row(part[...])
    note[2:3, :] = goal_row[...]
    note[3:4, :] = jnp.zeros_like(goal_row)


def combine(own, peer, pair, inverse):
    inv = 1.0 / (own[0:1, :] + peer[1:2, :])
    inverse[...] = to_column(inv)
    pair[0:1, :] = inv
    pair[1:2, :] = own[2:3, :]
    pair[2:3, :] = 1.0 / (peer[0:1, :] + own[1:2, :])
    pair[3:4, :] = peer[2:3, :]


def seal(emb, relay, goal, e_in, total_in, pos_in, unit, rnorm, e_all, total, pos, *kept):
    add_block(4, emb, relay, goal, e_all, total, pos)


def lose(total, pos, losses, token):
    losses[...] = to_row(jnp.log(total[...]) - pos[...])
    token[...] = jnp.zeros_like(token)


def slope(e, inverse, their_inverse, left, right):
    weight = e * (inverse + their_inverse)
    return jnp.where(left == right, weight - 1.0, weight)


def finish(
    base, goal, inverse, pair, even_note, odd_note, e_all, emb, peer, even, odd, relay, unit, rnorm, token,
    dz, g, acc,
):
    at = places()
    pair, even_note, odd_note = pair[...], even_note[...], odd_note[...]
    relay_note = jnp.where(crossed(), even_note, odd_note)[2:]
    notes = (pair[:2], pair[2:], even_note[:2], odd_note[:2], relay_note)
    blocks = (emb, peer, even, odd, relay)
    half, size = g.shape[1:]
    ids = lax.broadcasted_iota(jnp.int32, (1, size), 1)

    def slopes(k, rows):
        note = notes[k]
        their_inverse, their_goal = note[0:1], note[1:2].astype(jnp.int32)
        shift = at[k] * size
        ahead = at[k] >= 0
        right = jnp.where(ahead, ids + shift, their_goal + shift)
        mine = lax.broadcasted_iota(jnp.int32, (rows.size, 1), 0) + rows.start
        left = jnp.where(ahead, goal[rows, :], mine)
        weight = slope(e_all[k, rows, :], inverse[rows, :], their_inverse, left, right)
        if k == 0:
            weight = jnp.where(mine == their_goal, weight - 1.0, weight)
        g[k % 2, here(rows), :] = weight.astype(BF16)

    def here(rows):
        return pl.ds(rows.start - base, rows.size)

    tiles = [pl.ds(base + r, TILE) for r in range(0, half, TILE)]
    for rows in tiles:
        slopes(0, rows)
    for k, block in enumerate(blocks):
        product = dot(g[k % 2], block[...])
        if k + 1 < len(blocks):
            for rows in tiles:
                slopes(k + 1, rows)
        if k == 0:
            acc[...] = product
        else:
            acc[...] += product
    for rows in tiles:
        demb = SCALE * acc[here(rows), :]
        u = unit[rows, :]
        along = jnp.sum(u * demb, axis=1, keepdims=True)
        dz[here(rows), :] = ((demb - u * along) * rnorm[rows, :]).astype(BF16)


def turn(frames, token, mine, theirs):
    half, core = mine.shape[0], lax.axis_index("core")
    for out, k in ((mine, core), (theirs, 1 - core)):
        for c in range(0, half, 256):
            columns = pl.ds(pl.multiple_of(k * half + c, 128), 256)
            out[pl.ds(c, 256), :] = frames[:, columns].T


def add_up(got, out):
    total = got[0].astype(F32)
    for k in range(1, got.shape[0]):
        total += got[k].astype(F32)
    total = total.astype(BF16)
    for k in range(out.shape[0]):
        out[k] = total


def head_first(mine, theirs, dz_a, dz_b, other_a, out):
    n = dz_a.shape[0]
    out[...] = dot(mine[:, :n], dz_a[...]) + dot(theirs[:, :n], other_a[...]) + dot(mine[:, n:], dz_b[...])


def head_last(part, theirs, other_b, out):
    cut, n = out.shape[2], other_b.shape[0]
    for r in range(0, out.shape[1], WIDE):
        rows = pl.ds(r, WIDE)
        whole = part[rows, :] + dot(theirs[rows, n:], other_b[...])
        for k in range(2):
            out[k, rows, :] = whole[:, k * cut : (k + 1) * cut].astype(BF16)


def half_copies(part, out, sems, core):
    _, size, cut = part.shape
    step = size // 2
    start = pl.multiple_of(core * size, size)
    return [
        pltpu.make_async_copy(
            part.at[k, pl.ds(r * step, step), :],
            out.at[pl.ds(start + r * step, step), pl.ds(k * cut, cut)],
            sems.at[k, r],
        )
        for k in range(2)
        for r in range(2)
    ]


def ends(dz_a, dz_b, head, own, frame_grad, out, held, sems, out_sems):
    copies = half_copies(own, out, sems, lax.axis_index("core"))
    for c in copies:
        c.start()
    step = head.shape[0] // out_sems.shape[0]
    for k in range(out_sems.shape[0]):
        cut = pl.ds(k * step, step)
        n = dz_a.shape[0]
        held[:n, cut] = dot_nt(dz_a[...], head[cut, :]).astype(BF16)
        held[n:, cut] = dot_nt(dz_b[...], head[cut, :]).astype(BF16)
        copies.append(pltpu.make_async_copy(held.at[:, cut], frame_grad.at[:, cut], out_sems.at[k]))
        copies[-1].start()
    for c in copies:
        c.wait()


def last_half(other, whole, out, sems):
    copies = half_copies(other, out, sems, 1 - lax.axis_index("core"))
    for c in copies:
        c.start()
    for c in copies:
        c.wait()


def on_device(frames, head, offsets):
    rows, depth = frames.shape
    width = head.shape[1]
    shape = jax.ShapeDtypeStruct
    col, row = shape((rows, 1), F32), shape((1, rows), F32)
    square, tall = shape((rows, rows), F32), shape((rows, width), F32)
    note = shape((2, rows), F32)
    block_flops = 2 * rows * rows * width
    half = depth // 2
    vmem, hbm = pl.BlockSpec(memory_space=pltpu.VMEM), pl.BlockSpec(memory_space=pltpu.HBM)
    emb, unit, rnorm = pl.pallas_call(
        embed,
        in_specs=[hbm, hbm],
        out_specs=[vmem] * 3,
        out_shape=[shape((rows, width), BF16), tall, col],
        scratch_shapes=[
            pltpu.VMEM((rows, depth), BF16),
            pltpu.VMEM((depth, width), BF16),
            pltpu.VMEM((rows, width), F32),
            pltpu.SemaphoreType.DMA((2, 2)),
        ],
        name="embed",
        compiler_params=pltpu.CompilerParams(vmem_limit_bytes=51 * 2**20),
        cost_estimate=pl.CostEstimate(flops=2 * rows * depth * width, bytes_accessed=2**22, transcendentals=0),
    )(frames, head)

    peer = in_chip(emb)
    odd = swap_odd(emb)
    even = swap_even(emb)
    everything = shape((5, rows, rows), F32)
    e_all, total, pos, unit, rnorm, goal, goal_row = call(
        near, [everything, col, col, tall, col, shape((rows, 1), jnp.int32), row],
        emb, peer, offsets.reshape(1, rows), unit, rnorm,
        kept=((3, 3), (4, 4)), flops=2 * block_flops, name="near",
    )
    mine, theirs = call(turn, [shape((half, rows), BF16)] * 2, frames, pos, name="turn")
    theirs = in_chip(theirs)
    state, keep = [everything, col, col, tall, col], lambda k: tuple((k + j, j) for j in range(5))
    note = shape((4, rows), F32)
    e_all, total, pos, unit, rnorm, own_note = call(
        far, state + [note], emb, even, odd, peer, goal, goal_row, theirs, e_all, total, pos, unit, rnorm,
        kept=keep(7), scratch=[pltpu.VMEM((rows, 1), F32)], flops=3 * block_flops, name="far",
    )
    peer_note = in_chip(own_note)
    pair, inverse = call(combine, [note, col], own_note, peer_note, name="combine")
    odd_note = swap_odd(pair)
    even_note = swap_even(pair)
    (shared,) = call(pick, [shape((rows, width), BF16)], even, odd, theirs, name="pick")
    relay = in_chip(shared)
    e_all, total, pos, unit, rnorm = call(
        seal, state, emb, relay, goal, e_all, total, pos, unit, rnorm, kept=keep(3), flops=block_flops, name="seal",
    )
    losses, token = call(lose, [row, shape((8, 128), F32)], total, pos, name="lose")
    parts = []
    for base in (0, rows // 2):
        (dz,) = call(
            functools.partial(finish, base), [shape((rows // 2, width), BF16)], goal, inverse, pair, even_note, odd_note,
            e_all, emb, peer, even, odd, relay, unit, rnorm, token,
            scratch=[pltpu.VMEM((2, rows // 2, rows), BF16), pltpu.VMEM((rows // 2, width), F32)],
            flops=5 * block_flops // 2, name="finish",
        )
        parts.append(dz)
        token = dz
    others = [in_chip(dz) for dz in parts]

    flops = 2 * half * rows * width
    (partial,) = call(
        head_first, [shape((half, width), F32)], mine, theirs, *parts, others[0], flops=flops, name="head_first"
    )
    (partial,) = call(
        head_last, [shape((2, half, width // 2), BF16)], partial, theirs, others[1], flops=flops, name="head_last"
    )
    share = (half // 16, width // 2)
    got = lax.all_to_all(partial.reshape(32, *share), NEAR, split_axis=0, concat_axis=0)
    (copies,) = call(add_up, [shape((4, *share), BF16)], got, name="add_near")
    got = lax.all_to_all(copies, "zh", split_axis=0, concat_axis=0)
    (copies,) = call(add_up, [shape((32, *share), BF16)], got, name="add_far")
    own = lax.all_to_all(copies, NEAR, split_axis=0, concat_axis=0).reshape(2, half, width // 2)
    other = in_chip(own)
    anywhere = pl.BlockSpec(memory_space=pl.ANY)
    frame_grad, head_grad = pl.pallas_call(
        ends,
        in_specs=[vmem, vmem, vmem, anywhere],
        out_specs=[anywhere] * 2,
        out_shape=[shape((rows, depth), BF16), shape((depth, width), BF16)],
        scratch_shapes=[
            pltpu.VMEM((rows, depth), BF16), pltpu.SemaphoreType.DMA((2, 2)), pltpu.SemaphoreType.DMA((3,))
        ],
        name="ends",
        compiler_params=pltpu.CompilerParams(vmem_limit_bytes=16 * 2**20),
        cost_estimate=pl.CostEstimate(flops=2 * rows * depth * width, bytes_accessed=2**22, transcendentals=0),
    )(*parts, head, own)
    head_grad = pl.pallas_call(
        last_half,
        in_specs=[anywhere] * 2,
        out_specs=anywhere,
        out_shape=shape((depth, width), BF16),
        scratch_shapes=[pltpu.SemaphoreType.DMA((2, 2))],
        input_output_aliases={1: 0},
        name="last_half",
        compiler_params=pltpu.CompilerParams(vmem_limit_bytes=2**20),
    )(other, head_grad)
    return (losses.reshape(rows), frame_grad, head_grad)


def solution(mesh):
    torus = Mesh(mesh.devices.reshape(SIZES), ALL)
    return jax.shard_map(
        on_device,
        mesh=torus,
        in_specs=(P(ALL, None), P(), P(ALL)),
        out_specs=(P(ALL), P(ALL, None), P()),
        check_vma=False,
    )
```

```python
import functools

import jax
import jax.numpy as jnp
from jax import lax
from jax.experimental import pallas as pl
from jax.experimental.pallas import tpu as pltpu
from jax.sharding import Mesh, PartitionSpec as P

SCALE = 50.0
ALL = ("zh", "zl", "y", "x", "core")
SIZES = (4, 2, 4, 4, 2)
NEAR = ("zl", "y", "x")
F32, BF16 = jnp.float32, jnp.bfloat16
TILE, WIDE = 128, 256


def send(x, to):
    return lax.ppermute(x, ALL, [(i, to(i) % 256) for i in range(256)])


def in_chip(x):
    return send(x, lambda i: i ^ 1)


def swap_even(x):
    return send(x, lambda i: i ^ 2)


def swap_odd(x):
    return send(x, lambda i: ((i + 2) ^ 2) - 2)


def dot(left, right):
    return jnp.dot(left, right, preferred_element_type=F32)


def dot_nt(left, right):
    return lax.dot_general(left, right, (((1,), (1,)), ((), ())), preferred_element_type=F32)


def to_row(column):
    return jnp.broadcast_to(column, (column.shape[0], 128)).T[:1]


def to_column(row):
    return jnp.broadcast_to(row, (128, row.shape[1])).T[:, :1]


def call(body, out, *arrays, scratch=(), flops=0, name=None, kept=()):
    vmem = pl.BlockSpec(memory_space=pltpu.VMEM)
    size = sum(a.size * a.dtype.itemsize for a in (*arrays, *out))
    return pl.pallas_call(
        body,
        out_shape=out,
        in_specs=[vmem] * len(arrays),
        out_specs=[vmem] * len(out),
        scratch_shapes=scratch,
        input_output_aliases=dict(kept),
        name=name,
        compiler_params=pltpu.CompilerParams(vmem_limit_bytes=16 * 2**20),
        cost_estimate=pl.CostEstimate(flops=flops, bytes_accessed=size, transcendentals=0),
    )(*arrays)


def embed(frames, head, emb, unit, rnorm, f, h, acc, sems):
    depth = head.shape[0]
    cuts = (pl.ds(0, depth // 2), pl.ds(depth // 2, depth // 2))
    copies = []
    for k, cut in enumerate(cuts):
        copies.append(pltpu.make_async_copy(frames.at[:, cut], f.at[:, cut], sems.at[0, k]))
        copies.append(pltpu.make_async_copy(head.at[cut, :], h.at[cut, :], sems.at[1, k]))
    for c in copies:
        c.start()
    copies[0].wait()
    copies[1].wait()
    acc[...] = dot(f[:, cuts[0]], h[cuts[0], :])
    copies[2].wait()
    copies[3].wait()
    cut = cuts[1]
    for r in range(0, acc.shape[0], WIDE):
        rows = pl.ds(r, WIDE)
        z = acc[rows, :] + dot(f[rows, cut], h[cut, :])
        norm = jnp.sqrt(jnp.sum(z * z, axis=1, keepdims=True) + 1e-06)
        inverse = 1.0 / norm
        u = z * inverse
        unit[rows, :] = u
        emb[rows, :] = u.astype(BF16)
        rnorm[rows, :] = inverse


def chip_sign():
    return 1 - 2 * lax.rem(lax.axis_index("x"), 2)


def crossed():
    return lax.rem(lax.axis_index("x") + lax.axis_index("core"), 2) == 1


def places():
    core = 1 - 2 * lax.axis_index("core")
    return (0, core, 2 * chip_sign(), -2 * chip_sign(), -core)


def pick(even, odd, token, out):
    out[...] = even[...]

    @pl.when(crossed())
    def _():
        out[...] = odd[...]


def score_tile(at, emb, block, goal, rows):
    score = SCALE * dot_nt(emb[rows, :], block[...])
    cols = lax.broadcasted_iota(jnp.int32, score.shape, 1) + at * block.shape[0]
    hit = cols == goal[rows, :]
    return score, jnp.sum(jnp.where(hit, score, 0.0), axis=1, keepdims=True)


def near(emb, peer, offsets, unit, rnorm, e_all, total, pos, unit_out, rnorm_out, goal, goal_row):
    at = places()
    positives = (offsets[...] + lax.broadcasted_iota(jnp.int32, offsets.shape, 1)).astype(F32)
    goal_row[...] = positives
    goal[...] = to_column(positives).astype(jnp.int32)
    for r in range(0, emb.shape[0], WIDE):
        rows = pl.ds(r, WIDE)
        score, p0 = score_tile(0, emb, emb, goal, rows)
        e = jnp.exp(score)
        i = lax.broadcasted_iota(jnp.int32, e.shape, 0) + r
        e = jnp.where(i == lax.broadcasted_iota(jnp.int32, e.shape, 1), 0.0, e)
        e_all[0, rows, :] = e
        total[rows, :] = jnp.sum(e, axis=1, keepdims=True)
        score, p1 = score_tile(at[1], emb, peer, goal, rows)
        e = jnp.exp(score)
        e_all[1, rows, :] = e
        total[rows, :] += jnp.sum(e, axis=1, keepdims=True)
        pos[rows, :] = p0 + p1


def add_block(slot, emb, block, goal, e_all, total, pos):
    at = places()[slot]
    for r in range(0, emb.shape[0], WIDE):
        rows = pl.ds(r, WIDE)
        score, p = score_tile(at, emb, block, goal, rows)
        e = jnp.exp(score)
        e_all[slot, rows, :] = e
        total[rows, :] += jnp.sum(e, axis=1, keepdims=True)
        pos[rows, :] += p


def far(
    emb, odd, even, peer, goal, goal_row, token, e_in, total_in, pos_in, unit, rnorm,
    e_all, total, pos, unit_out, rnorm_out, note, part,
):
    def for_peer(block):
        for r in range(0, peer.shape[0], WIDE):
            rows = pl.ds(r, WIDE)
            e = jnp.exp(SCALE * dot_nt(peer[rows, :], block[...]))
            part[rows, :] = jnp.sum(e, axis=1, keepdims=True)

    pl.when(crossed())(lambda: for_peer(odd))
    pl.when(jnp.logical_not(crossed()))(lambda: for_peer(even))
    add_block(2, emb, even, goal, e_all, total, pos)
    add_block(3, emb, odd, goal, e_all, total, pos)
    note[0:1, :] = to_row(total[...])
    note[1:2, :] = to_row(part[...])
    note[2:3, :] = goal_row[...]
    note[3:4, :] = jnp.zeros_like(goal_row)


def combine(own, peer, pair, inverse):
    inv = 1.0 / (own[0:1, :] + peer[1:2, :])
    inverse[...] = to_column(inv)
    pair[0:1, :] = inv
    pair[1:2, :] = own[2:3, :]
    pair[2:3, :] = 1.0 / (peer[0:1, :] + own[1:2, :])
    pair[3:4, :] = peer[2:3, :]


def seal(emb, relay, goal, e_in, total_in, pos_in, unit, rnorm, e_all, total, pos, *kept):
    add_block(4, emb, relay, goal, e_all, total, pos)


def lose(total, pos, losses, token):
    losses[...] = to_row(jnp.log(total[...]) - pos[...])
    token[...] = jnp.zeros_like(token)


def slope(e, inverse, their_inverse, left, right):
    weight = e * (inverse + their_inverse)
    return jnp.where(left == right, weight - 1.0, weight)


def finish(
    base, goal, inverse, pair, even_note, odd_note, e_all, emb, peer, even, odd, relay, unit, rnorm, token,
    dz, g, acc,
):
    at = places()
    pair, even_note, odd_note = pair[...], even_note[...], odd_note[...]
    relay_note = jnp.where(crossed(), even_note, odd_note)[2:]
    notes = (pair[:2], pair[2:], even_note[:2], odd_note[:2], relay_note)
    blocks = (emb, peer, even, odd, relay)
    half, size = g.shape[1:]
    ids = lax.broadcasted_iota(jnp.int32, (1, size), 1)

    def slopes(k, rows):
        note = notes[k]
        their_inverse, their_goal = note[0:1], note[1:2].astype(jnp.int32)
        shift = at[k] * size
        ahead = at[k] >= 0
        right = jnp.where(ahead, ids + shift, their_goal + shift)
        mine = lax.broadcasted_iota(jnp.int32, (rows.size, 1), 0) + rows.start
        left = jnp.where(ahead, goal[rows, :], mine)
        weight = slope(e_all[k, rows, :], inverse[rows, :], their_inverse, left, right)
        if k == 0:
            weight = jnp.where(mine == their_goal, weight - 1.0, weight)
        g[k % 2, here(rows), :] = weight.astype(BF16)

    def here(rows):
        return pl.ds(rows.start - base, rows.size)

    tiles = [pl.ds(base + r, TILE) for r in range(0, half, TILE)]
    for rows in tiles:
        slopes(0, rows)
    for k, block in enumerate(blocks):
        product = dot(g[k % 2], block[...])
        if k + 1 < len(blocks):
            for rows in tiles:
                slopes(k + 1, rows)
        if k == 0:
            acc[...] = product
        else:
            acc[...] += product
    for rows in tiles:
        demb = SCALE * acc[here(rows), :]
        u = unit[rows, :]
        along = jnp.sum(u * demb, axis=1, keepdims=True)
        dz[here(rows), :] = ((demb - u * along) * rnorm[rows, :]).astype(BF16)


def turn(frames, token, mine, theirs):
    half, core = mine.shape[0], lax.axis_index("core")
    for out, k in ((mine, core), (theirs, 1 - core)):
        for c in range(0, half, 256):
            columns = pl.ds(pl.multiple_of(k * half + c, 128), 256)
            out[pl.ds(c, 256), :] = frames[:, columns].T


def add_up(got, out):
    total = got[0].astype(F32)
    for k in range(1, got.shape[0]):
        total += got[k].astype(F32)
    total = total.astype(BF16)
    for k in range(out.shape[0]):
        out[k] = total


def head_first(mine, theirs, dz_a, dz_b, other_a, out):
    n = dz_a.shape[0]
    out[...] = dot(mine[:, :n], dz_a[...]) + dot(theirs[:, :n], other_a[...]) + dot(mine[:, n:], dz_b[...])


def head_last(part, theirs, other_b, out):
    cut, n = out.shape[2], other_b.shape[0]
    for r in range(0, out.shape[1], WIDE):
        rows = pl.ds(r, WIDE)
        whole = part[rows, :] + dot(theirs[rows, n:], other_b[...])
        for k in range(2):
            out[k, rows, :] = whole[:, k * cut : (k + 1) * cut].astype(BF16)


def half_copies(part, out, sems, core):
    _, size, cut = part.shape
    step = size // 2
    start = pl.multiple_of(core * size, size)
    return [
        pltpu.make_async_copy(
            part.at[k, pl.ds(r * step, step), :],
            out.at[pl.ds(start + r * step, step), pl.ds(k * cut, cut)],
            sems.at[k, r],
        )
        for k in range(2)
        for r in range(2)
    ]


def ends(dz_a, dz_b, head, own, frame_grad, out, held, sems, out_sems):
    copies = half_copies(own, out, sems, lax.axis_index("core"))
    for c in copies:
        c.start()
    step = head.shape[0] // out_sems.shape[0]
    for k in range(out_sems.shape[0]):
        cut = pl.ds(k * step, step)
        n = dz_a.shape[0]
        held[:n, cut] = dot_nt(dz_a[...], head[cut, :]).astype(BF16)
        held[n:, cut] = dot_nt(dz_b[...], head[cut, :]).astype(BF16)
        copies.append(pltpu.make_async_copy(held.at[:, cut], frame_grad.at[:, cut], out_sems.at[k]))
        copies[-1].start()
    for c in copies:
        c.wait()


def last_half(other, whole, out, sems):
    copies = half_copies(other, out, sems, 1 - lax.axis_index("core"))
    for c in copies:
        c.start()
    for c in copies:
        c.wait()


def on_device(frames, head, offsets):
    rows, depth = frames.shape
    width = head.shape[1]
    shape = jax.ShapeDtypeStruct
    col, row = shape((rows, 1), F32), shape((1, rows), F32)
    square, tall = shape((rows, rows), F32), shape((rows, width), F32)
    note = shape((2, rows), F32)
    block_flops = 2 * rows * rows * width
    half = depth // 2
    vmem, hbm = pl.BlockSpec(memory_space=pltpu.VMEM), pl.BlockSpec(memory_space=pltpu.HBM)
    emb, unit, rnorm = pl.pallas_call(
        embed,
        in_specs=[hbm, hbm],
        out_specs=[vmem] * 3,
        out_shape=[shape((rows, width), BF16), tall, col],
        scratch_shapes=[
            pltpu.VMEM((rows, depth), BF16),
            pltpu.VMEM((depth, width), BF16),
            pltpu.VMEM((rows, width), F32),
            pltpu.SemaphoreType.DMA((2, 2)),
        ],
        name="embed",
        compiler_params=pltpu.CompilerParams(vmem_limit_bytes=51 * 2**20),
        cost_estimate=pl.CostEstimate(flops=2 * rows * depth * width, bytes_accessed=2**22, transcendentals=0),
    )(frames, head)

    peer = in_chip(emb)
    odd = swap_odd(emb)
    even = swap_even(emb)
    everything = shape((5, rows, rows), F32)
    e_all, total, pos, unit, rnorm, goal, goal_row = call(
        near, [everything, col, col, tall, col, shape((rows, 1), jnp.int32), row],
        emb, peer, offsets.reshape(1, rows), unit, rnorm,
        kept=((3, 3), (4, 4)), flops=2 * block_flops, name="near",
    )
    mine, theirs = call(turn, [shape((half, rows), BF16)] * 2, frames, pos, name="turn")
    theirs = in_chip(theirs)
    state, keep = [everything, col, col, tall, col], lambda k: tuple((k + j, j) for j in range(5))
    note = shape((4, rows), F32)
    e_all, total, pos, unit, rnorm, own_note = call(
        far, state + [note], emb, odd, even, peer, goal, goal_row, theirs, e_all, total, pos, unit, rnorm,
        kept=keep(7), scratch=[pltpu.VMEM((rows, 1), F32)], flops=3 * block_flops, name="far",
    )
    peer_note = in_chip(own_note)
    pair, inverse = call(combine, [note, col], own_note, peer_note, name="combine")
    odd_note = swap_odd(pair)
    even_note = swap_even(pair)
    (shared,) = call(pick, [shape((rows, width), BF16)], even, odd, pair, name="pick")
    relay = in_chip(shared)
    e_all, total, pos, unit, rnorm = call(
        seal, state, emb, relay, goal, e_all, total, pos, unit, rnorm, kept=keep(3), flops=block_flops, name="seal",
    )
    losses, token = call(lose, [row, shape((8, 128), F32)], total, pos, name="lose")
    parts = []
    for base in (0, rows // 2):
        (dz,) = call(
            functools.partial(finish, base), [shape((rows // 2, width), BF16)], goal, inverse, pair, even_note, odd_note,
            e_all, emb, peer, even, odd, relay, unit, rnorm, token,
            scratch=[pltpu.VMEM((2, rows // 2, rows), BF16), pltpu.VMEM((rows // 2, width), F32)],
            flops=5 * block_flops // 2, name="finish",
        )
        parts.append(dz)
        token = dz
    others = [in_chip(dz) for dz in parts]

    flops = 2 * half * rows * width
    (partial,) = call(
        head_first, [shape((half, width), F32)], mine, theirs, *parts, others[0], flops=flops, name="head_first"
    )
    (partial,) = call(
        head_last, [shape((2, half, width // 2), BF16)], partial, theirs, others[1], flops=flops, name="head_last"
    )
    share = (half // 16, width // 2)
    got = lax.all_to_all(partial.reshape(32, *share), NEAR, split_axis=0, concat_axis=0)
    (copies,) = call(add_up, [shape((4, *share), BF16)], got, name="add_near")
    got = lax.all_to_all(copies, "zh", split_axis=0, concat_axis=0)
    (copies,) = call(add_up, [shape((32, *share), BF16)], got, name="add_far")
    own = lax.all_to_all(copies, NEAR, split_axis=0, concat_axis=0).reshape(2, half, width // 2)
    other = in_chip(own)
    anywhere = pl.BlockSpec(memory_space=pl.ANY)
    frame_grad, head_grad = pl.pallas_call(
        ends,
        in_specs=[vmem, vmem, vmem, anywhere],
        out_specs=[anywhere] * 2,
        out_shape=[shape((rows, depth), BF16), shape((depth, width), BF16)],
        scratch_shapes=[
            pltpu.VMEM((rows, depth), BF16), pltpu.SemaphoreType.DMA((2, 2)), pltpu.SemaphoreType.DMA((3,))
        ],
        name="ends",
        compiler_params=pltpu.CompilerParams(vmem_limit_bytes=16 * 2**20),
        cost_estimate=pl.CostEstimate(flops=2 * rows * depth * width, bytes_accessed=2**22, transcendentals=0),
    )(*parts, head, own)
    head_grad = pl.pallas_call(
        last_half,
        in_specs=[anywhere] * 2,
        out_specs=anywhere,
        out_shape=shape((depth, width), BF16),
        scratch_shapes=[pltpu.SemaphoreType.DMA((2, 2))],
        input_output_aliases={1: 0},
        name="last_half",
        compiler_params=pltpu.CompilerParams(vmem_limit_bytes=2**20),
    )(other, head_grad)
    return (losses.reshape(rows), frame_grad, head_grad)


def solution(mesh):
    torus = Mesh(mesh.devices.reshape(SIZES), ALL)
    return jax.shard_map(
        on_device,
        mesh=torus,
        in_specs=(P(ALL, None), P(), P(ALL)),
        out_specs=(P(ALL), P(ALL, None), P()),
        check_vma=False,
    )
```
